256 devices in a mesh: mem: 32 (over z, x), obs: 8 (over y, core).
Axes of the slice: x: 4, y: 4, z: 8, core: 2. Of those that a mesh axis runs over, the one named last changes fastest.
Arguments:
- members: bfloat16 [2048, 4096], P(('mem', 'obs')), may hold values from -9 to 9
- alphas: int32 [8, 4096], replicated, may hold values from 0 to 3
- obs_inputs: float32 [8, 1024], replicated, may hold values from -1 to 1
- block_ids: int32 [1024], P('obs'), may hold values from 0 to 3
- noise_var: float32 [1024], P('obs'), may hold values from 0.5 to 4
- observed: float32 [1024], P('obs'), may hold values from -18 to 18
- perturb: bfloat16 [2048, 1024], P('mem', 'obs'), may hold values from -6 to 6
Outputs:
- updated: float32 [2048, 4096], P(('mem', 'obs'))
The draws below stay inside these ranges and needn't reach their ends.
All inputs are finite; a program needn't handle non-finite values.
Results may differ from the reference program's by a relative error of at most 0.0035.
Values may be sent and summed in bfloat16 or wider, within the bound.
A program may use at most 256 MiB of HBM per device.

```python
import math
import jax
import jax.numpy as jnp
from jax import lax

COEFFS = 4096
DIMS = 8
DEGREE = 3
BLOCKS = 4
TILE_OBS = 128
ENSEMBLE = 2048
OBSERV = 1024
N_OBS = 8


def draw_members(key, part):
    centre_key = jax.random.fold_in(key, 17)
    spread_key = jax.random.fold_in(key, 29)
    centre = jnp.clip(1.5 * jax.random.normal(centre_key, (COEFFS,), jnp.float32), -4.5, 4.5)
    spread = jnp.clip(jax.random.normal(spread_key, (ENSEMBLE, COEFFS), jnp.float32), -4.5, 4.5)
    return (centre[None, :] + spread).astype(jnp.bfloat16)


def set_ends(entries, own_key, low, high):
    shape = entries.shape
    spot = [jax.random.randint(jax.random.fold_in(own_key, axis), (), 0, shape[axis]) for axis in range(len(shape))]
    entries = entries.at[tuple(spot)].set(low)
    longest = shape.index(max(shape))
    spot[longest] = (spot[longest] + 1) % shape[longest]
    return entries.at[tuple(spot)].set(high)


def shard_levels(key, extent, pieces, least, largest):
    def one(axis_at, blocks):
        draws = jax.random.uniform(jax.random.fold_in(jax.random.fold_in(key, 6), axis_at), (blocks,), jnp.float32, least / len(pieces), largest / len(pieces))
        return jnp.repeat(jnp.exp(draws), extent[axis_at] // blocks).reshape((-1,) + (1,) * (len(extent) - axis_at - 1))

    level = one(*pieces[0])
    for cut in pieces[1:]:
        level = level * one(*cut)
    return level


def bell_draw(key, extent, scale, limit, pieces=(), kind=jnp.bfloat16):
    values = scale * jax.random.normal(key, extent, jnp.float32)
    if pieces:
        values = values * shard_levels(key, extent, pieces, -0.22, 0.18)
    return jnp.clip(values, -limit, limit).astype(kind)


def setup_inputs(seed: int = 0) -> dict:
    splits = jax.random.split(jax.random.key(seed), 8)
    members = draw_members(jax.random.fold_in(splits[7], 71), 0)
    alphas = set_ends(jax.random.randint(splits[1], (DIMS, COEFFS), 0, DEGREE + 1), jax.random.fold_in(splits[1], 1), 0, DEGREE).astype(jnp.int32)
    obs_inputs = jnp.clip(jax.random.uniform(splits[2], (DIMS, OBSERV), jnp.float32, -1.0, 1.0), -1.0, 1.0)
    block_ids = set_ends(jax.random.randint(splits[3], (OBSERV,), 0, BLOCKS), jax.random.fold_in(splits[3], 1), 0, BLOCKS - 1).astype(jnp.int32)
    noise_var = jnp.clip(jnp.exp(math.log(4.0) - 2.0794415 * jax.random.uniform(splits[4], (OBSERV,), jnp.float32) ** shard_levels(splits[4], (OBSERV,), ((0, 8),), -0.2, 0.2)), 0.5, 4.0)
    observed = bell_draw(splits[5], (OBSERV,), 3.0, 18.0, ((0, 8),), jnp.float32)
    perturb = bell_draw(splits[6], (ENSEMBLE, OBSERV), 1.0, 6.0, ((0, 32), (1, 8)))
    return {"members": members, "alphas": alphas, "obs_inputs": obs_inputs, "block_ids": block_ids, "noise_var": noise_var, "observed": observed, "perturb": perturb}


def hermite_table(points):
    values = [jnp.ones_like(points), points]
    for degree in range(1, DEGREE):
        values.append(points * values[degree] - degree * values[degree - 1])
    return jnp.stack([values[term_degree] * (1.0 / math.sqrt(math.factorial(term_degree))) for term_degree in range(DEGREE + 1)], axis=0)

def reference(members, alphas, obs_inputs, block_ids, noise_var, observed, perturb):
    hermite = hermite_table(obs_inputs)
    product = None
    for dim_index in range(DIMS):
        picked = jnp.take(hermite[:, dim_index, :], alphas[dim_index], axis=0)
        product = picked if product is None else product * picked
    basis = product.T.astype(jnp.bfloat16)
    predicted = jnp.dot(members.astype(jnp.float32), basis.T.astype(jnp.float32), preferred_element_type=jnp.float32).astype(jnp.bfloat16)
    mean_param = lax.optimization_barrier(jnp.sum(members, axis=0, dtype=jnp.float32)) / ENSEMBLE
    mean_pred = lax.optimization_barrier(jnp.sum(predicted, axis=0, dtype=jnp.float32)) / ENSEMBLE
    cross_cov = jnp.dot(members.T.astype(jnp.float32), predicted.astype(jnp.float32), preferred_element_type=jnp.float32) - ENSEMBLE * mean_param[:, None] * mean_pred[None, :]
    pred_gram = jnp.dot(predicted.T.astype(jnp.float32), predicted.astype(jnp.float32), preferred_element_type=jnp.float32) - ENSEMBLE * mean_pred[:, None] * mean_pred[None, :]
    innovation = observed[None, :] + jnp.sqrt(noise_var)[None, :] * perturb.astype(jnp.float32) - predicted.astype(jnp.float32)

    def solve_tile(tile_index):
        tile_start = (tile_index * TILE_OBS).astype(jnp.int32)
        gram_tile = lax.dynamic_slice(pred_gram, (tile_start, tile_start), (TILE_OBS, TILE_OBS))
        labels = lax.dynamic_slice_in_dim(block_ids, tile_start, TILE_OBS)
        variance = lax.dynamic_slice_in_dim(noise_var, tile_start, TILE_OBS)
        system = jnp.where(labels[:, None] == labels[None, :], gram_tile / (ENSEMBLE - 1), 0.0) + jnp.diag(variance)
        right_side = lax.dynamic_slice_in_dim(innovation, tile_start, TILE_OBS, 1)
        return jnp.linalg.solve(system, right_side.T)
    solved = lax.map(solve_tile, jnp.arange(N_OBS, dtype=jnp.int32)).reshape(OBSERV, ENSEMBLE)
    increment = jnp.dot(solved.T.astype(jnp.float32), cross_cov.T.astype(jnp.float32), precision=lax.Precision.HIGHEST, preferred_element_type=jnp.float32) / (ENSEMBLE - 1)
    return members.astype(jnp.float32) + increment
```

```python
import math

import jax
import jax.numpy as jnp
from jax import lax
from jax.experimental import pallas as pl
from jax.experimental.pallas import tpu as pltpu
from jax.sharding import PartitionSpec as P

ROWS = 8
TILE = 128
SLAB = 128
PANEL = 8
CHUNK = 256
F32 = jnp.float32
BF16 = jnp.bfloat16
FIRST = (((0,), (0,)), ((), ()))
LAST = (((1,), (1,)), ((), ()))
PLAIN = (((1,), (0,)), ((), ()))


def dot(left, right, dims, precision=None):
    return lax.dot_general(left, right, dims, precision=precision, preferred_element_type=F32)


def inverse(matrix):
    size = matrix.shape[0]
    row = lax.broadcasted_iota(jnp.int32, (PANEL, size), 0)
    lane = lax.broadcasted_iota(jnp.int32, (PANEL, size), 1)
    rest_lane = lax.broadcasted_iota(jnp.int32, (size - PANEL, size), 1)
    unit = jnp.where(lane == row, 1.0, 0.0).astype(F32)

    def block(_, full):
        top, rest = full[:PANEL], full[PANEL:]
        column = [jnp.broadcast_to(top[:, j : j + 1], (PANEL, size)) for j in range(PANEL)]
        panel = jnp.where(lane < PANEL, unit, top)
        for p in range(PANEL):
            scale = 1.0 / column[p][p : p + 1]
            pivot = panel[p : p + 1] * scale
            panel = jnp.where(row == p, pivot, panel - column[p] * pivot)
            for j in range(p + 1, PANEL):
                entry = column[j][p : p + 1] * scale
                column[j] = jnp.where(row == p, entry, column[j] - column[p] * entry)
        update = jnp.where(rest_lane < PANEL, 0.0, rest)
        for j in range(PANEL):
            update = update - rest[:, j : j + 1] * panel[j : j + 1]
        return pltpu.roll(jnp.concatenate([update, panel], axis=0), size - PANEL, 1)

    return lax.fori_loop(0, size // PANEL, block, matrix)


def kernel(
    nm,
    no,
    members,
    alphas,
    points,
    labels,
    noise,
    observed,
    perturb,
    out,
    rows,
    blocks_out,
    blocks_in,
    slabs,
    preds,
    perts,
    table,
    basis,
    innov,
    share_out,
    prior,
    incr_out,
    incr_in,
    final,
    coupled,
    spread,
    rows_s,
    rows_r,
    blocks_s,
    blocks_r,
    slabs_s,
    slabs_r,
    preds_s,
    preds_r,
    perts_s,
    perts_r,
    share_s,
    share_r,
    incr_s,
    incr_r,
):
    g, o = lax.axis_index("mem"), lax.axis_index("obs")
    y, c = lax.div(o, 2), lax.rem(o, 2)
    ny = no // 2
    coeffs = members.shape[1]
    half = coeffs // 2
    ensemble = nm * no * ROWS
    side = nm * ROWS

    def mem_peer(d):
        return lax.rem(g + d, nm)

    def obs_peer(d):
        return lax.rem(o + d, no)

    def y_peer(d):
        return lax.rem(y + d, ny) * 2 + c

    sibling = y * 2 + 1 - c

    def copy(src, dst, send, recv, to):
        return pltpu.make_async_remote_copy(
            src_ref=src, dst_ref=dst, send_sem=send, recv_sem=recv, device_id=to, device_id_type=pl.DeviceIdType.MESH
        )

    barrier = pltpu.get_barrier_semaphore()

    def greet_mem(d, carry):
        pl.semaphore_signal(barrier, inc=1, device_id=(mem_peer(d), o), device_id_type=pl.DeviceIdType.MESH)
        return carry

    def greet_obs(d, carry):
        pl.semaphore_signal(barrier, inc=1, device_id=(g, obs_peer(d)), device_id_type=pl.DeviceIdType.MESH)
        return carry

    lax.fori_loop(1, no, greet_obs, 0)
    lax.fori_loop(1, nm, greet_mem, 0)

    own = members[...].astype(F32)
    rows[o] = jnp.concatenate([own[:, :half], own[:, half:]], axis=0).astype(BF16)
    for k in range(nm):
        blocks_out[k] = own[:, k * SLAB : (k + 1) * SLAB]
    blocks_in[g] = blocks_out[g]
    perts[g] = perturb[...]

    at = points[:, pl.ds(pl.multiple_of(o * TILE, TILE), TILE)]
    turned = jnp.concatenate([at, jnp.zeros((TILE - at.shape[0], TILE), F32)], axis=0).T
    for d in range(at.shape[0]):
        x = jnp.broadcast_to(turned[:, d : d + 1], (TILE, TILE))
        second = x * x - 1.0
        third = x * second - 2.0 * x
        table[d, 0] = x
        table[d, 1] = second * (1.0 / math.sqrt(2.0))
        table[d, 2] = third * (1.0 / math.sqrt(6.0))

    label = jnp.broadcast_to(labels[...].astype(F32), (TILE, TILE))
    diagonal = lax.broadcasted_iota(jnp.int32, (TILE, TILE), 0) == lax.broadcasted_iota(jnp.int32, (TILE, TILE), 1)
    coupled[...] = jnp.where(label == label.T, 1.0 / (ensemble - 1), 0.0).astype(F32)
    spread[...] = jnp.where(diagonal, jnp.broadcast_to(noise[...], (TILE, TILE)), 0.0)

    pl.semaphore_wait(barrier, nm + no - 2)

    def send_rows(d):
        return copy(rows.at[o], rows.at[o], rows_s.at[d], rows_r.at[o], (g, y_peer(d)))

    def pass_rows(d):
        at = y_peer(d)
        return copy(rows.at[at], rows.at[at], rows_s.at[ny + d], rows_r.at[at], (g, sibling))

    own_rows = copy(rows.at[o], rows.at[o], rows_s.at[0], rows_r.at[o], (g, sibling))

    def take_rows(at):
        copy(rows.at[at], rows.at[at], rows_s.at[0], rows_r.at[at], (g, sibling)).wait_recv()

    for d in range(1, ny):
        send_rows(d).start()
    own_rows.start()

    def send_block(d):
        to = mem_peer(d)
        return copy(blocks_out.at[to], blocks_in.at[g], blocks_s.at[d], blocks_r.at[g], (to, o))

    def take_block(d):
        at = mem_peer(d)
        copy(blocks_out.at[at], blocks_in.at[at], blocks_s.at[d], blocks_r.at[at], (at, o)).wait_recv()

    def each(count, act):
        def step(d, carry):
            act(d)
            return carry

        lax.fori_loop(1, count, step, 0)

    each(nm, lambda d: send_block(d).start())

    def basis_chunk(part):
        def step(t, carry):
            first = pl.multiple_of(t * CHUNK, CHUNK)
            degree = alphas[:, pl.ds(pl.multiple_of(part * half + first, CHUNK), CHUNK)]
            product = None
            for d in range(degree.shape[0]):
                odd = (degree[d : d + 1] & 1) == 1
                high = degree[d : d + 1] >= 2
                one, two, three = (jnp.concatenate([table[d, q]] * (CHUNK // TILE), axis=1) for q in range(3))
                value = jnp.where(high, jnp.where(odd, three, two), jnp.where(odd, one, 1.0))
                product = value if product is None else product * value
            basis[pl.ds(part * TILE, TILE), pl.ds(first, CHUNK)] = product.astype(BF16)
            return carry

        lax.fori_loop(0, half // CHUNK, step, 0)

    basis_chunk(0)
    for d in range(1, ny):
        take_rows(y_peer(d))
        pass_rows(d).start()
    basis_chunk(1)
    take_rows(sibling)
    for d in range(1, ny):
        take_rows(lax.rem(y + d, ny) * 2 + 1 - c)

    both = dot(rows[...].reshape(no * 2 * ROWS, half), basis[...], LAST)
    both = both.reshape(no, 2, ROWS, 2 * TILE)
    mine = (both[:, 0, :, :TILE] + both[:, 1, :, TILE:]).reshape(no * ROWS, TILE)
    preds[g] = mine.astype(BF16)

    def send_pred(d):
        return copy(preds.at[g], preds.at[g], preds_s.at[d], preds_r.at[g], (mem_peer(d), o))

    def take_pred(d):
        at = mem_peer(d)
        copy(preds.at[at], preds.at[at], preds_s.at[d], preds_r.at[at], (at, o)).wait_recv()

    def send_pert(d):
        return copy(perts.at[g], perts.at[g], perts_s.at[d], perts_r.at[g], (mem_peer(d), o))

    def take_pert(d):
        at = mem_peer(d)
        copy(perts.at[at], perts.at[at], perts_s.at[d], perts_r.at[at], (at, o)).wait_recv()

    each(nm, lambda d: send_pred(d).start())

    each(nm, take_block)
    slabs[o] = blocks_in[...].reshape(side, SLAB).astype(BF16)

    def send_slab(d):
        return copy(slabs.at[o], slabs.at[o], slabs_s.at[d], slabs_r.at[o], (g, y_peer(d)))

    def pass_slab(d):
        at = y_peer(d)
        return copy(slabs.at[at], slabs.at[at], slabs_s.at[ny + d], slabs_r.at[at], (g, sibling))

    own_slab = copy(slabs.at[o], slabs.at[o], slabs_s.at[0], slabs_r.at[o], (g, sibling))

    def take_slab(at):
        copy(slabs.at[at], slabs.at[at], slabs_s.at[0], slabs_r.at[at], (g, sibling)).wait_recv()

    for d in range(1, ny):
        send_slab(d).start()
    own_slab.start()
    each(nm, lambda d: send_pert(d).start())

    each(nm, take_pred)
    flat = preds[...].reshape(ensemble, TILE)
    ones = jnp.ones((2 * ROWS, ensemble), BF16)
    mean_pred = jnp.broadcast_to(dot(ones, flat, PLAIN)[:1] / ensemble, (TILE, TILE))
    mean_turned = mean_pred.T
    gram = dot(flat, flat, FIRST) - ensemble * mean_turned * mean_pred
    system = gram * coupled[...] + spread[...]

    for d in range(1, ny):
        take_slab(y_peer(d))
        pass_slab(d).start()

    inverted = inverse(system)

    each(nm, take_pert)
    noise_root = jnp.sqrt(noise[...])

    def innovate(t, carry):
        value = preds[t].astype(F32)
        left = observed[...] + noise_root * perts[t].astype(F32) - value
        for k in range(no):
            innov[k, pl.ds(pl.multiple_of(t * ROWS, ROWS), ROWS), :] = left[k * ROWS : (k + 1) * ROWS]
            prior[k, pl.ds(pl.multiple_of(t * ROWS, ROWS), ROWS), :] = value[k * ROWS : (k + 1) * ROWS]
        return carry

    lax.fori_loop(0, nm, innovate, 0)
    ordered = prior[...].reshape(ensemble, TILE).astype(BF16)

    take_slab(sibling)
    for d in range(1, ny):
        take_slab(lax.rem(y + d, ny) * 2 + 1 - c)
    slab = slabs[...].reshape(ensemble, SLAB)
    mean_param = jnp.broadcast_to(dot(ones, slab, PLAIN)[:1] / ensemble, (TILE, SLAB))
    cross = dot(ordered, slab, FIRST) - ensemble * mean_turned * mean_param
    gain = dot(inverted, cross, PLAIN, lax.Precision.HIGHEST) / (ensemble - 1)
    high = gain.astype(BF16)
    low = (gain - high.astype(F32)).astype(BF16)
    weights = jnp.concatenate([high, low], axis=1)
    weights = jnp.concatenate([weights, weights], axis=0)

    def send_share(d):
        to = obs_peer(d)
        return copy(share_out.at[to], incr_in.at[o], share_s.at[d], share_r.at[o], (g, to))

    def take_share(d):
        at = obs_peer(d)
        copy(share_out.at[at], incr_in.at[at], share_s.at[d], share_r.at[at], (g, at)).wait_recv()

    def share(at):
        left = innov[at]
        big = left.astype(BF16)
        small = (left - big.astype(F32)).astype(BF16)
        parts = dot(jnp.concatenate([big, small], axis=1), weights, PLAIN)
        return parts[:, :SLAB] + parts[:, SLAB:]

    for d in range(1, no):
        to = obs_peer(d)
        share_out[to] = share(to).astype(BF16)
        send_share(d).start()
    total = share(o)
    for d in range(1, no):
        take_share(d)
        total = total + incr_in[obs_peer(d)].astype(F32)
    incr_out[...] = total.reshape(nm, ROWS, SLAB)

    def send_incr(d):
        to = mem_peer(d)
        return copy(incr_out.at[to], final.at[g], incr_s.at[d], incr_r.at[g], (to, o))

    def take_incr(d):
        at = mem_peer(d)
        copy(incr_out.at[at], final.at[at], incr_s.at[d], incr_r.at[at], (at, o)).wait_recv()

    each(nm, lambda d: send_incr(d).start())
    final[g] = incr_out[g]
    each(nm, take_incr)
    for k in range(nm):
        out[:, k * SLAB : (k + 1) * SLAB] = own[:, k * SLAB : (k + 1) * SLAB] + final[k]

    for d in range(1, ny):
        send_rows(d).wait_send()
        pass_rows(d).wait_send()
        send_slab(d).wait_send()
        pass_slab(d).wait_send()
    own_rows.wait_send()
    own_slab.wait_send()
    for d in range(1, no):
        send_share(d).wait_send()

    def sent(d):
        send_block(d).wait_send()
        send_pred(d).wait_send()
        send_pert(d).wait_send()
        send_incr(d).wait_send()

    each(nm, sent)


def shards(members, alphas, points, labels, noise, observed, perturb):
    nm, no = lax.axis_size("mem"), lax.axis_size("obs")
    coeffs = members.shape[1]
    side = nm * ROWS
    vmem = pl.BlockSpec(memory_space=pltpu.VMEM)
    many = pltpu.SemaphoreType.DMA
    return pl.pallas_call(
        lambda *refs: kernel(nm, no, *refs),
        out_shape=jax.ShapeDtypeStruct((ROWS, coeffs), F32),
        in_specs=[vmem] * 7,
        out_specs=vmem,
        scratch_shapes=[
            pltpu.VMEM((no, 2 * ROWS, coeffs // 2), BF16),
            pltpu.VMEM((nm, ROWS, SLAB), F32),
            pltpu.VMEM((nm, ROWS, SLAB), F32),
            pltpu.VMEM((no, side, SLAB), BF16),
            pltpu.VMEM((nm, no * ROWS, TILE), BF16),
            pltpu.VMEM((nm, no * ROWS, TILE), BF16),
            pltpu.VMEM((alphas.shape[0], 3, TILE, TILE), F32),
            pltpu.VMEM((2 * TILE, coeffs // 2), BF16),
            pltpu.VMEM((no, side, TILE), F32),
            pltpu.VMEM((no, side, SLAB), BF16),
            pltpu.VMEM((no, side, TILE), F32),
            pltpu.VMEM((nm, ROWS, SLAB), F32),
            pltpu.VMEM((no, side, SLAB), BF16),
            pltpu.VMEM((nm, ROWS, SLAB), F32),
            pltpu.VMEM((TILE, TILE), F32),
            pltpu.VMEM((TILE, TILE), F32),
            many((no,)),
            many((no,)),
            many((nm,)),
            many((nm,)),
            many((no,)),
            many((no,)),
            many((nm,)),
            many((nm,)),
            many((nm,)),
            many((nm,)),
            many((no,)),
            many((no,)),
            many((nm,)),
            many((nm,)),
        ],
        compiler_params=pltpu.CompilerParams(
            collective_id=0, has_side_effects=True, vmem_limit_bytes=40 * 1024 * 1024
        ),
    )(members, alphas, points, labels.reshape(1, TILE), noise.reshape(1, TILE), observed.reshape(1, TILE), perturb)


def solution(mesh):
    in_specs = (P(("mem", "obs"), None), P(), P(), P("obs"), P("obs"), P("obs"), P("mem", "obs"))
    out_specs = P(("mem", "obs"), None)
    return jax.shard_map(shards, mesh=mesh, in_specs=in_specs, out_specs=out_specs, check_vma=False)
```

```python
import math

import jax
import jax.numpy as jnp
from jax import lax
from jax.experimental import pallas as pl
from jax.experimental.pallas import tpu as pltpu
from jax.sharding import PartitionSpec as P

ROWS = 8
TILE = 128
SLAB = 128
PANEL = 8
CHUNK = 256
NX = 4
F32 = jnp.float32
BF16 = jnp.bfloat16
FIRST = (((0,), (0,)), ((), ()))
LAST = (((1,), (1,)), ((), ()))
PLAIN = (((1,), (0,)), ((), ()))


def dot(left, right, dims, precision=None):
    return lax.dot_general(left, right, dims, precision=precision, preferred_element_type=F32)


def inverse(matrix):
    size = matrix.shape[0]
    row = lax.broadcasted_iota(jnp.int32, (PANEL, size), 0)
    lane = lax.broadcasted_iota(jnp.int32, (PANEL, size), 1)
    rest_lane = lax.broadcasted_iota(jnp.int32, (size - PANEL, size), 1)
    unit = jnp.where(lane == row, 1.0, 0.0).astype(F32)

    def block(_, full):
        top, rest = full[:PANEL], full[PANEL:]
        column = [jnp.broadcast_to(top[:, j : j + 1], (PANEL, size)) for j in range(PANEL)]
        panel = jnp.where(lane < PANEL, unit, top)
        for p in range(PANEL):
            scale = 1.0 / column[p][p : p + 1]
            pivot = panel[p : p + 1] * scale
            panel = jnp.where(row == p, pivot, panel - column[p] * pivot)
            for j in range(p + 1, PANEL):
                entry = column[j][p : p + 1] * scale
                column[j] = jnp.where(row == p, entry, column[j] - column[p] * entry)
        update = jnp.where(rest_lane < PANEL, 0.0, rest)
        for j in range(PANEL):
            update = update - rest[:, j : j + 1] * panel[j : j + 1]
        return pltpu.roll(jnp.concatenate([update, panel], axis=0), size - PANEL, 1)

    return lax.fori_loop(0, size // PANEL, block, matrix)


def kernel(
    nm,
    no,
    members_hbm,
    alphas_hbm,
    points_hbm,
    labels_hbm,
    noise_hbm,
    observed_hbm,
    perturb_hbm,
    out,
    members,
    alphas,
    points,
    labels,
    noise,
    observed,
    rows_out,
    rows_in,
    halves,
    half_in,
    blocks_out,
    blocks_in,
    slabs,
    preds,
    perts,
    grams,
    table,
    basis,
    innov,
    prior,
    pair_out,
    pair_in,
    share_out,
    share_in,
    incr_out,
    final,
    coupled,
    spread,
    local_s,
    rows_s,
    rows_r,
    half_s,
    half_r,
    blocks_s,
    blocks_r,
    slabs_s,
    slabs_r,
    preds_s,
    preds_r,
    lines_s,
    lines_r,
    perts_s,
    perts_r,
    extra_s,
    extra_r,
    grams_s,
    grams_r,
    pair_s,
    pair_r,
    share_s,
    share_r,
    incr_s,
    incr_r,
):
    g, o = lax.axis_index("mem"), lax.axis_index("obs")
    z, x = lax.div(g, NX), lax.rem(g, NX)
    y, c = lax.div(o, 2), lax.rem(o, 2)
    nz, ny = nm // NX, no // 2
    coeffs = members.shape[1]
    half = coeffs // 2
    quarter = half // 2
    chunk = min(CHUNK, quarter)
    ensemble = nm * no * ROWS
    line = nz * no * ROWS
    side = nm * ROWS
    slot = x * nz + z
    mesh = pl.DeviceIdType.MESH

    def mem_at(d):
        return lax.rem(g + d, nm)

    def slot_at(at):
        return lax.rem(at, NX) * nz + lax.div(at, NX)

    def obs_at(d):
        return lax.rem(o + d, no)

    def z_at(d):
        return lax.rem(z + d, nz)

    def x_at(d):
        return lax.rem(x + d, NX)

    def y_at(d):
        return lax.rem(y + d, ny)

    sibling = y * 2 + 1 - c

    def copy(src, dst, send, recv, to):
        return pltpu.make_async_remote_copy(
            src_ref=src, dst_ref=dst, send_sem=send, recv_sem=recv, device_id=to, device_id_type=mesh
        )

    def each(count, act):
        def step(d, carry):
            act(d)
            return carry

        lax.fori_loop(1, count, step, 0)

    fetch = [
        pltpu.make_async_copy(src, dst, local_s.at[k])
        for k, (src, dst) in enumerate(
            (
                (members_hbm, members),
                (points_hbm.at[:, pl.ds(pl.multiple_of(y * 2 * TILE, 2 * TILE), 2 * TILE)], points),
                (labels_hbm, labels),
                (noise_hbm, noise),
                (observed_hbm, observed),
                (perturb_hbm, perts.at[slot]),
                (alphas_hbm, alphas),
            )
        )
    ]
    for f in fetch:
        f.start()

    barrier = pltpu.get_barrier_semaphore()
    each(no, lambda d: pl.semaphore_signal(barrier, inc=1, device_id=(g, obs_at(d)), device_id_type=mesh))
    each(nm, lambda d: pl.semaphore_signal(barrier, inc=1, device_id=(mem_at(d), o), device_id_type=mesh))

    fetch[0].wait()
    own = members[...].astype(F32)
    for h in range(2):
        part = own[:, h * half : (h + 1) * half]
        rows_out[h] = jnp.concatenate([part[:, :quarter], part[:, quarter:]], axis=0).astype(BF16)
    rows_in[o] = rows_out[c]
    for k in range(nm):
        blocks_out[k] = own[:, k * SLAB : (k + 1) * SLAB]
    blocks_in[slot] = blocks_out[g]

    fetch[1].wait()
    for t in range(2):
        at = points[:, t * TILE : (t + 1) * TILE]
        turned = jnp.concatenate([at, jnp.zeros((TILE - at.shape[0], TILE), F32)], axis=0).T
        for d in range(at.shape[0]):
            value = jnp.broadcast_to(turned[:, d : d + 1], (TILE, TILE))
            second = value * value - 1.0
            third = value * second - 2.0 * value
            table[t, d, 0] = value
            table[t, d, 1] = second * (1.0 / math.sqrt(2.0))
            table[t, d, 2] = third * (1.0 / math.sqrt(6.0))

    for f in fetch[2:]:
        f.wait()
    label = jnp.broadcast_to(labels[...].astype(F32), (TILE, TILE))
    diagonal = lax.broadcasted_iota(jnp.int32, (TILE, TILE), 0) == lax.broadcasted_iota(jnp.int32, (TILE, TILE), 1)
    coupled[...] = jnp.where(label == label.T, 1.0 / (ensemble - 1), 0.0).astype(F32)
    spread[...] = jnp.where(diagonal, jnp.broadcast_to(noise[...], (TILE, TILE)), 0.0)

    pl.semaphore_wait(barrier, nm + no - 2)

    def rows_to(d):
        to = obs_at(d)
        return copy(rows_out.at[lax.rem(to, 2)], rows_in.at[o], rows_s.at[d], rows_r.at[o], (g, to))

    def rows_from(d):
        at = obs_at(d)
        return copy(rows_out.at[c], rows_in.at[at], rows_s.at[d], rows_r.at[at], (g, at))

    each(no, lambda d: rows_to(d).start())

    def pert_to(d):
        return copy(perts.at[slot], perts.at[slot], perts_s.at[d], perts_r.at[z], (z_at(d) * NX + x, o))

    def pert_from(d):
        at = x * nz + z_at(d)
        return copy(perts.at[at], perts.at[at], perts_s.at[d], perts_r.at[z_at(d)], (z_at(d) * NX + x, o))

    each(nz, lambda d: pert_to(d).start())

    def block_to(d):
        to = mem_at(d)
        return copy(blocks_out.at[to], blocks_in.at[slot], blocks_s.at[d], blocks_r.at[slot], (to, o))

    def block_from(d):
        at = mem_at(d)
        place = slot_at(at)
        return copy(blocks_out.at[at], blocks_in.at[place], blocks_s.at[d], blocks_r.at[place], (at, o))

    each(nm, lambda d: block_to(d).start())

    def basis_part(q):
        def step(n, carry):
            t, k = lax.div(n, quarter // chunk), lax.rem(n, quarter // chunk)
            first = pl.multiple_of(k * chunk, chunk)
            degree = alphas[:, pl.ds(pl.multiple_of(c * half + q * quarter + first, chunk), chunk)]
            product = None
            for d in range(degree.shape[0]):
                odd = (degree[d : d + 1] & 1) == 1
                high = degree[d : d + 1] >= 2
                one, two, three = (jnp.concatenate([table[t, d, p]] * (chunk // TILE), axis=1) for p in range(3))
                value = jnp.where(high, jnp.where(odd, three, two), jnp.where(odd, one, 1.0))
                product = value if product is None else product * value
            place = pl.multiple_of((q * 2 + t) * TILE, TILE)
            basis[pl.ds(place, TILE), pl.ds(first, chunk)] = product.astype(BF16)
            return carry

        lax.fori_loop(0, 2 * (quarter // chunk), step, 0)

    def line_to(buffer, send, recv, d):
        span = buffer.at[pl.ds(x * nz, nz)]
        return copy(span, span, send.at[d], recv.at[x], (z * NX + x_at(d), o))

    def line_from(buffer, send, recv, d):
        span = buffer.at[pl.ds(x_at(d) * nz, nz)]
        return copy(span, span, send.at[d], recv.at[x_at(d)], (z * NX + x_at(d), o))

    basis_part(0)
    each(nz, lambda d: pert_from(d).wait_recv())
    each(NX, lambda d: line_to(perts, extra_s, extra_r, d).start())
    basis_part(1)

    each(no, lambda d: rows_from(d).wait_recv())
    both = dot(rows_in[...].reshape(no * 2 * ROWS, quarter), basis[...], LAST)
    both = both.reshape(no, 2, ROWS, 4 * TILE)
    part = (both[:, 0, :, : 2 * TILE] + both[:, 1, :, 2 * TILE :]).reshape(no * ROWS, 2 * TILE)
    for t in range(2):
        halves[t] = part[:, t * TILE : (t + 1) * TILE]
    half_copy = copy(halves.at[1 - c], half_in, half_s, half_r, (g, sibling))
    half_copy.start()
    half_copy.wait_recv()
    preds[slot] = (halves[c] + half_in[...]).astype(BF16)

    def pred_to(d):
        return copy(preds.at[slot], preds.at[slot], preds_s.at[d], preds_r.at[z], (z_at(d) * NX + x, o))

    def pred_from(d):
        at = x * nz + z_at(d)
        return copy(preds.at[at], preds.at[at], preds_s.at[d], preds_r.at[z_at(d)], (z_at(d) * NX + x, o))

    each(nz, lambda d: pred_to(d).start())

    each(nm, lambda d: block_from(d).wait_recv())
    slabs[o] = blocks_in[...].reshape(side, SLAB).astype(BF16)

    def slab_to(d):
        return copy(slabs.at[o], slabs.at[o], slabs_s.at[d], slabs_r.at[o], (g, y_at(d) * 2 + c))

    def slab_from(at, to):
        return copy(slabs.at[at], slabs.at[at], slabs_s.at[0], slabs_r.at[at], (g, to))

    def slab_pass(d):
        at = y_at(d) * 2 + c
        return copy(slabs.at[at], slabs.at[at], slabs_s.at[ny + d], slabs_r.at[at], (g, sibling))

    slab_own = copy(slabs.at[o], slabs.at[o], slabs_s.at[0], slabs_r.at[o], (g, sibling))
    each(ny, lambda d: slab_to(d).start())
    slab_own.start()

    each(nz, lambda d: pred_from(d).wait_recv())
    flat = preds[pl.ds(x * nz, nz)].reshape(line, TILE)
    ones = jnp.ones((2 * ROWS, ensemble), BF16)
    grams[x, :TILE] = dot(flat, flat, FIRST)
    grams[x, TILE:] = dot(ones[:, :line], flat, PLAIN)[:ROWS]

    def gram_to(d):
        return copy(grams.at[x], grams.at[x], grams_s.at[d], grams_r.at[x], (z * NX + x_at(d), o))

    def gram_from(d):
        at = x_at(d)
        return copy(grams.at[at], grams.at[at], grams_s.at[d], grams_r.at[at], (z * NX + at, o))

    each(NX, lambda d: gram_to(d).start())
    each(NX, lambda d: line_to(preds, lines_s, lines_r, d).start())

    def pass_on(d):
        at = y_at(d) * 2 + c
        slab_from(at, at).wait_recv()
        slab_pass(d).start()

    each(ny, pass_on)

    each(NX, lambda d: gram_from(d).wait_recv())
    gram = grams[0]
    for k in range(1, NX):
        gram = gram + grams[k]
    mean_pred = jnp.broadcast_to(gram[TILE : TILE + 1] / ensemble, (TILE, TILE))
    mean_turned = mean_pred.T
    system = (gram[:TILE] - ensemble * mean_turned * mean_pred) * coupled[...] + spread[...]

    inverted = inverse(system)

    each(NX, lambda d: line_from(perts, extra_s, extra_r, d).wait_recv())
    each(NX, lambda d: line_from(preds, lines_s, lines_r, d).wait_recv())
    noise_root = jnp.sqrt(noise[...])

    def innovate(t, carry):
        value = preds[t].astype(F32)
        left = observed[...] + noise_root * perts[t].astype(F32) - value
        place = pl.ds(pl.multiple_of(t * ROWS, ROWS), ROWS)
        for k in range(no):
            innov[k, place, :] = left[k * ROWS : (k + 1) * ROWS]
            prior[k, place, :] = value[k * ROWS : (k + 1) * ROWS]
        return carry

    lax.fori_loop(0, nm, innovate, 0)
    ordered = prior[...].reshape(ensemble, TILE).astype(BF16)

    slab_from(sibling, sibling).wait_recv()
    each(ny, lambda d: slab_from(y_at(d) * 2 + 1 - c, sibling).wait_recv())
    slab = slabs[...].reshape(ensemble, SLAB)
    mean_param = jnp.broadcast_to(dot(ones, slab, PLAIN)[:1] / ensemble, (TILE, SLAB))
    cross = dot(ordered, slab, FIRST) - ensemble * mean_turned * mean_param
    gain = dot(inverted, cross, PLAIN, lax.Precision.HIGHEST) / (ensemble - 1)
    high = gain.astype(BF16)
    low = (gain - high.astype(F32)).astype(BF16)
    weights = jnp.concatenate([high, low], axis=1)
    weights = jnp.concatenate([weights, weights], axis=0)

    def share(at):
        left = innov[at]
        big = left.astype(BF16)
        small = (left - big.astype(F32)).astype(BF16)
        parts = dot(jnp.concatenate([big, small], axis=1), weights, PLAIN)
        return parts[:, :SLAB] + parts[:, SLAB:]

    def pair_copy(d):
        at = y_at(d)
        return copy(pair_out.at[d], pair_in.at[d], pair_s.at[d], pair_r.at[d], (g, sibling))

    def share_to(d):
        return copy(share_out.at[d], share_in.at[y], share_s.at[d], share_r.at[y], (g, y_at(d) * 2 + c))

    def share_from(d):
        at = y_at(d)
        return copy(share_out.at[d], share_in.at[at], share_s.at[d], share_r.at[at], (g, at * 2 + c))

    turns = sorted(range(1, ny), key=lambda d: -min(d, ny - d)) + [0]
    for d in turns:
        pair_out[d] = share(y_at(d) * 2 + 1 - c).astype(BF16)
        pair_copy(d).start()
    for d in turns:
        total = share(y_at(d) * 2 + c)
        pair_copy(d).wait_recv()
        total = total + pair_in[d].astype(F32)
        if d:
            share_out[d] = total.astype(BF16)
            share_to(d).start()
    for d in turns[:-1]:
        share_from(d).wait_recv()
        total = total + share_in[y_at(d)].astype(F32)
    incr_out[...] = total.reshape(nm, ROWS, SLAB)

    def incr_to(d):
        to = mem_at(d)
        return copy(incr_out.at[slot_at(to)], final.at[g], incr_s.at[d], incr_r.at[g], (to, o))

    def incr_from(d):
        at = mem_at(d)
        return copy(incr_out.at[slot_at(at)], final.at[at], incr_s.at[d], incr_r.at[at], (at, o))

    each(nm, lambda d: incr_to(d).start())
    final[g] = incr_out[slot]
    each(nm, lambda d: incr_from(d).wait_recv())
    for k in range(nm):
        at = slice(k * SLAB, (k + 1) * SLAB)
        out[:, at] = members[:, at].astype(F32) + final[k]

    def obs_sent(d):
        rows_to(d).wait_send()

    def y_sent(d):
        slab_to(d).wait_send()
        slab_pass(d).wait_send()
        share_to(d).wait_send()
        pair_copy(d).wait_send()

    def z_sent(d):
        pert_to(d).wait_send()
        pred_to(d).wait_send()

    def x_sent(d):
        gram_to(d).wait_send()
        line_to(perts, extra_s, extra_r, d).wait_send()
        line_to(preds, lines_s, lines_r, d).wait_send()

    def mem_sent(d):
        block_to(d).wait_send()
        incr_to(d).wait_send()

    half_copy.wait_send()
    slab_own.wait_send()
    pair_copy(0).wait_send()
    each(no, obs_sent)
    each(ny, y_sent)
    each(nz, z_sent)
    each(NX, x_sent)
    each(nm, mem_sent)


def shards(members, alphas, points, labels, noise, observed, perturb):
    nm, no = lax.axis_size("mem"), lax.axis_size("obs")
    nz, ny = nm // NX, no // 2
    coeffs = members.shape[1]
    dims = alphas.shape[0]
    side = nm * ROWS
    vmem, many = pltpu.VMEM, pltpu.SemaphoreType.DMA
    return pl.pallas_call(
        lambda *refs: kernel(nm, no, *refs),
        out_shape=jax.ShapeDtypeStruct((ROWS, coeffs), F32),
        in_specs=[pl.BlockSpec(memory_space=pl.ANY)] * 7,
        out_specs=pl.BlockSpec(memory_space=vmem),
        scratch_shapes=[
            vmem((ROWS, coeffs), BF16),
            vmem((dims, coeffs), jnp.int32),
            vmem((dims, 2 * TILE), F32),
            vmem((1, TILE), jnp.int32),
            vmem((1, TILE), F32),
            vmem((1, TILE), F32),
            vmem((2, 2 * ROWS, coeffs // 4), BF16),
            vmem((no, 2 * ROWS, coeffs // 4), BF16),
            vmem((2, no * ROWS, TILE), F32),
            vmem((no * ROWS, TILE), F32),
            vmem((nm, ROWS, SLAB), F32),
            vmem((nm, ROWS, SLAB), F32),
            vmem((no, side, SLAB), BF16),
            vmem((nm, no * ROWS, TILE), BF16),
            vmem((nm, no * ROWS, TILE), BF16),
            vmem((NX, TILE + ROWS, TILE), F32),
            vmem((2, dims, 3, TILE, TILE), F32),
            vmem((4 * TILE, coeffs // 4), BF16),
            vmem((no, side, TILE), F32),
            vmem((no, side, TILE), F32),
            vmem((ny, side, SLAB), BF16),
            vmem((ny, side, SLAB), BF16),
            vmem((ny, side, SLAB), BF16),
            vmem((ny, side, SLAB), BF16),
            vmem((nm, ROWS, SLAB), F32),
            vmem((nm, ROWS, SLAB), F32),
            vmem((TILE, TILE), F32),
            vmem((TILE, TILE), F32),
            many((7,)),
            many((no,)),
            many((no,)),
            many,
            many,
            many((nm,)),
            many((nm,)),
            many((no,)),
            many((no,)),
            many((nz,)),
            many((nz,)),
            many((NX,)),
            many((NX,)),
            many((nz,)),
            many((nz,)),
            many((NX,)),
            many((NX,)),
            many((NX,)),
            many((NX,)),
            many((ny,)),
            many((ny,)),
            many((ny,)),
            many((ny,)),
            many((nm,)),
            many((nm,)),
        ],
        compiler_params=pltpu.CompilerParams(
            collective_id=0, has_side_effects=True, vmem_limit_bytes=60 * 1024 * 1024
        ),
    )(members, alphas, points, labels.reshape(1, TILE), noise.reshape(1, TILE), observed.reshape(1, TILE), perturb)


def solution(mesh):
    in_specs = (P(("mem", "obs"), None), P(), P(), P("obs"), P("obs"), P("obs"), P("mem", "obs"))
    out_specs = P(("mem", "obs"), None)
    return jax.shard_map(shards, mesh=mesh, in_specs=in_specs, out_specs=out_specs, check_vma=False)
```

```python
import math

import jax
import jax.numpy as jnp
from jax import lax
from jax.experimental import pallas as pl
from jax.experimental.pallas import tpu as pltpu
from jax.sharding import PartitionSpec as P

ROWS = 8
TILE = 128
SLAB = 128
PANEL = 8
CHUNK = 256
NX = 4
F32 = jnp.float32
BF16 = jnp.bfloat16
FIRST = (((0,), (0,)), ((), ()))
LAST = (((1,), (1,)), ((), ()))
PLAIN = (((1,), (0,)), ((), ()))


def dot(left, right, dims, precision=None):
    return lax.dot_general(left, right, dims, precision=precision, preferred_element_type=F32)


def inverse_blocks(matrix, first, last):
    size = matrix.shape[0]
    row = lax.broadcasted_iota(jnp.int32, (PANEL, size), 0)
    lane = lax.broadcasted_iota(jnp.int32, (PANEL, size), 1)
    rest_lane = lax.broadcasted_iota(jnp.int32, (size - PANEL, size), 1)
    unit = jnp.where(lane == row, 1.0, 0.0).astype(F32)

    def block(_, full):
        top, rest = full[:PANEL], full[PANEL:]
        column = [jnp.broadcast_to(top[:, j : j + 1], (PANEL, size)) for j in range(PANEL)]
        panel = jnp.where(lane < PANEL, unit, top)
        for p in range(PANEL):
            scale = 1.0 / column[p][p : p + 1]
            pivot = panel[p : p + 1] * scale
            panel = jnp.where(row == p, pivot, panel - column[p] * pivot)
            for j in range(p + 1, PANEL):
                entry = column[j][p : p + 1] * scale
                column[j] = jnp.where(row == p, entry, column[j] - column[p] * entry)
        update = jnp.where(rest_lane < PANEL, 0.0, rest)
        for j in range(PANEL):
            update = update - rest[:, j : j + 1] * panel[j : j + 1]
        return pltpu.roll(jnp.concatenate([update, panel], axis=0), size - PANEL, 1)

    return lax.fori_loop(first, last, block, matrix)


def kernel(
    nm,
    no,
    members_hbm,
    alphas_hbm,
    points_hbm,
    labels_hbm,
    noise_hbm,
    observed_hbm,
    perturb_hbm,
    out,
    members,
    alphas,
    points,
    labels,
    noise,
    observed,
    rows_out,
    rows_in,
    halves,
    half_in,
    blocks_out,
    blocks_in,
    slabs,
    preds,
    perts,
    grams,
    table,
    basis,
    innov,
    prior,
    cross_out,
    cross_in,
    crosses,
    mine,
    pair_out,
    pair_in,
    share_out,
    share_in,
    incr_out,
    final,
    coupled,
    spread,
    right_r,
    left_r,
    local_s,
    rows_s,
    rows_r,
    half_s,
    half_r,
    blocks_s,
    blocks_r,
    slabs_s,
    slabs_r,
    preds_s,
    preds_r,
    perts_s,
    perts_r,
    grams_s,
    grams_r,
    cross_s,
    cross_r,
    crosses_s,
    crosses_r,
    pair_s,
    pair_r,
    share_s,
    share_r,
    incr_s,
    incr_r,
):
    g, o = lax.axis_index("mem"), lax.axis_index("obs")
    z, x = lax.div(g, NX), lax.rem(g, NX)
    y, c = lax.div(o, 2), lax.rem(o, 2)
    nz, ny = nm // NX, no // 2
    coeffs = members.shape[1]
    half = coeffs // 2
    quarter = half // 2
    width = coeffs // nz
    chunk = min(CHUNK, quarter)
    ensemble = nm * no * ROWS
    line = nz * no * ROWS
    side = nz * ROWS
    mesh = pl.DeviceIdType.MESH

    def obs_at(d):
        return lax.rem(o + d, no)

    def z_at(d):
        return lax.rem(z + d, nz)

    def x_at(d):
        return lax.rem(x + d, NX)

    def y_at(d):
        return lax.rem(y + d, ny)

    def in_z(at):
        return (at * NX + x, o)

    def in_x(at):
        return (z * NX + at, o)

    sibling = y * 2 + 1 - c

    def copy(src, dst, send, recv, to):
        return pltpu.make_async_remote_copy(
            src_ref=src, dst_ref=dst, send_sem=send, recv_sem=recv, device_id=to, device_id_type=mesh
        )

    def tell(semaphore, to):
        pl.semaphore_signal(semaphore, inc=1, device_id=to, device_id_type=mesh)

    def each(count, act):
        def step(d, carry):
            act(d)
            return carry

        lax.fori_loop(1, count, step, 0)

    fetch = [
        pltpu.make_async_copy(src, dst, local_s.at[k])
        for k, (src, dst) in enumerate(
            (
                (members_hbm, members),
                (points_hbm.at[:, pl.ds(pl.multiple_of(y * 2 * TILE, 2 * TILE), 2 * TILE)], points),
                (labels_hbm, labels),
                (noise_hbm, noise),
                (observed_hbm, observed),
                (perturb_hbm, perts.at[z]),
                (alphas_hbm, alphas),
            )
        )
    ]
    for f in fetch:
        f.start()

    barrier = pltpu.get_barrier_semaphore()
    after, before = z_at(1), z_at(nz - 1)
    each(no, lambda d: tell(barrier, (g, obs_at(d))))
    each(NX, lambda d: tell(barrier, in_x(x_at(d))))
    tell(barrier, in_z(after))
    tell(barrier, in_z(before))

    fetch[0].wait()
    own = members[...].astype(F32)
    for h in range(2):
        part = own[:, h * half : (h + 1) * half]
        rows_out[h] = jnp.concatenate([part[:, :quarter], part[:, quarter:]], axis=0).astype(BF16)
    rows_in[o] = rows_out[c]
    for k in range(nz):
        part = own[:, k * width : (k + 1) * width]
        blocks_out[k] = jnp.concatenate([part[:, : width // 2], part[:, width // 2 :]], axis=0).astype(BF16)
    blocks_in[z] = blocks_out[z]

    fetch[1].wait()
    for t in range(2):
        at = points[:, t * TILE : (t + 1) * TILE]
        turned = jnp.concatenate([at, jnp.zeros((TILE - at.shape[0], TILE), F32)], axis=0).T
        for d in range(at.shape[0]):
            value = jnp.broadcast_to(turned[:, d : d + 1], (TILE, TILE))
            second = value * value - 1.0
            third = value * second - 2.0 * value
            table[t, d, 0] = value
            table[t, d, 1] = second * (1.0 / math.sqrt(2.0))
            table[t, d, 2] = third * (1.0 / math.sqrt(6.0))

    pl.semaphore_wait(barrier, no - 1 + NX - 1 + 2)

    def rows_to(d):
        to = obs_at(d)
        return copy(rows_out.at[lax.rem(to, 2)], rows_in.at[o], rows_s.at[d], rows_r.at[o], (g, to))

    def rows_from(d):
        at = obs_at(d)
        return copy(rows_out.at[c], rows_in.at[at], rows_s.at[d], rows_r.at[at], (g, at))

    each(no, lambda d: rows_to(d).start())

    for f in fetch[2:]:
        f.wait()
    label = jnp.broadcast_to(labels[...].astype(F32), (TILE, TILE))
    diagonal = lax.broadcasted_iota(jnp.int32, (TILE, TILE), 0) == lax.broadcasted_iota(jnp.int32, (TILE, TILE), 1)
    coupled[...] = jnp.where(label == label.T, 1.0 / (ensemble - 1), 0.0).astype(F32)
    spread[...] = jnp.where(diagonal, jnp.broadcast_to(noise[...], (TILE, TILE)), 0.0)

    def basis_part(first_step, last_step):
        def step(n, carry):
            per = quarter // chunk
            q, t, k = lax.div(n, 2 * per), lax.rem(lax.div(n, per), 2), lax.rem(n, per)
            first = pl.multiple_of(k * chunk, chunk)
            degree = alphas[:, pl.ds(pl.multiple_of(c * half + q * quarter + first, chunk), chunk)]
            product = None
            for d in range(degree.shape[0]):
                odd = (degree[d : d + 1] & 1) == 1
                high = degree[d : d + 1] >= 2
                one, two, three = (jnp.concatenate([table[t, d, p]] * (chunk // TILE), axis=1) for p in range(3))
                value = jnp.where(high, jnp.where(odd, three, two), jnp.where(odd, one, 1.0))
                product = value if product is None else product * value
            place = pl.multiple_of((q * 2 + t) * TILE, TILE)
            basis[pl.ds(place, TILE), pl.ds(first, chunk)] = product.astype(BF16)
            return carry

        lax.fori_loop(first_step, last_step, step, 0)

    steps = 4 * (quarter // chunk)
    stages = nz // 2 - 1
    for k in range(stages):
        tell(right_r.at[k], in_z(after))
        tell(left_r.at[k], in_z(before))
        basis_part(steps * k // (stages + 1), steps * (k + 1) // (stages + 1))
        pl.semaphore_wait(right_r.at[k], 1)
        pl.semaphore_wait(left_r.at[k], 1)

    def block_to(d):
        return copy(blocks_out.at[z_at(d)], blocks_in.at[z], blocks_s.at[d], blocks_r.at[z], in_z(z_at(d)))

    def block_from(d):
        at = z_at(d)
        return copy(blocks_out.at[at], blocks_in.at[at], blocks_s.at[d], blocks_r.at[at], in_z(at))

    def pert_to(d):
        return copy(perts.at[z], perts.at[z], perts_s.at[d], perts_r.at[z], in_z(z_at(d)))

    def pert_from(d):
        at = z_at(d)
        return copy(perts.at[at], perts.at[at], perts_s.at[d], perts_r.at[at], in_z(at))

    each(nz, lambda d: block_to(d).start())
    each(nz, lambda d: pert_to(d).start())
    basis_part(steps * stages // (stages + 1), steps)

    each(no, lambda d: rows_from(d).wait_recv())
    both = dot(rows_in[...].reshape(no * 2 * ROWS, quarter), basis[...], LAST)
    both = both.reshape(no, 2, ROWS, 4 * TILE)
    part = (both[:, 0, :, : 2 * TILE] + both[:, 1, :, 2 * TILE :]).reshape(no * ROWS, 2 * TILE)
    for t in range(2):
        halves[t] = part[:, t * TILE : (t + 1) * TILE]
    half_copy = copy(halves.at[1 - c], half_in, half_s, half_r, (g, sibling))
    half_copy.start()
    half_copy.wait_recv()
    preds[z] = (halves[c] + half_in[...]).astype(BF16)

    def pred_to(d):
        return copy(preds.at[z], preds.at[z], preds_s.at[d], preds_r.at[z], in_z(z_at(d)))

    def pred_from(d):
        at = z_at(d)
        return copy(preds.at[at], preds.at[at], preds_s.at[d], preds_r.at[at], in_z(at))

    each(nz, lambda d: pred_to(d).start())

    each(nz, lambda d: block_from(d).wait_recv())
    block = blocks_in[...].astype(F32)
    block = jnp.concatenate([block[:, :ROWS], block[:, ROWS:]], axis=2)
    slabs[o] = block.reshape(side, width).astype(BF16)

    def slab_to(d):
        return copy(slabs.at[o], slabs.at[o], slabs_s.at[d], slabs_r.at[o], (g, y_at(d) * 2 + c))

    def slab_from(at, to):
        return copy(slabs.at[at], slabs.at[at], slabs_s.at[0], slabs_r.at[at], (g, to))

    def slab_pass(d):
        at = y_at(d) * 2 + c
        return copy(slabs.at[at], slabs.at[at], slabs_s.at[ny + d], slabs_r.at[at], (g, sibling))

    slab_own = copy(slabs.at[o], slabs.at[o], slabs_s.at[0], slabs_r.at[o], (g, sibling))
    each(ny, lambda d: slab_to(d).start())
    slab_own.start()

    each(nz, lambda d: pred_from(d).wait_recv())
    flat = preds[...].reshape(line, TILE)
    ones = jnp.ones((2 * ROWS, line), BF16)
    grams[x, :TILE] = dot(flat, flat, FIRST)
    grams[x, TILE:] = dot(ones, flat, PLAIN)[:ROWS]

    def gram_to(d):
        return copy(grams.at[x], grams.at[x], grams_s.at[d], grams_r.at[x], in_x(x_at(d)))

    def gram_from(d):
        at = x_at(d)
        return copy(grams.at[at], grams.at[at], grams_s.at[d], grams_r.at[at], in_x(at))

    each(NX, lambda d: gram_to(d).start())

    def pass_on(d):
        at = y_at(d) * 2 + c
        slab_from(at, at).wait_recv()
        slab_pass(d).start()

    each(ny, pass_on)

    each(nz, lambda d: pert_from(d).wait_recv())
    noise_root = jnp.sqrt(noise[...])
    for t in range(nz):
        value = preds[t].astype(F32)
        left = observed[...] + noise_root * perts[t].astype(F32) - value
        for k in range(no):
            prior[k, t * ROWS : (t + 1) * ROWS, :] = value[k * ROWS : (k + 1) * ROWS]
            innov[k % 2, k // 2, t * ROWS : (t + 1) * ROWS, :] = left[k * ROWS : (k + 1) * ROWS]
    ordered = prior[...].reshape(line, TILE).astype(BF16)

    slab_from(sibling, sibling).wait_recv()
    each(ny, lambda d: slab_from(y_at(d) * 2 + 1 - c, sibling).wait_recv())
    slab = slabs[...].reshape(line, width)
    raw = dot(ordered, slab, FIRST)
    total = dot(ones, slab, PLAIN)[:ROWS]
    for k in range(NX):
        cross_out[k, :TILE] = raw[:, k * SLAB : (k + 1) * SLAB]
        cross_out[k, TILE:] = total[:, k * SLAB : (k + 1) * SLAB]
    cross_in[x] = cross_out[x]

    def cross_to(d):
        at = x_at(d)
        return copy(cross_out.at[at], cross_in.at[x], cross_s.at[d], cross_r.at[x], in_x(at))

    def cross_from(d):
        at = x_at(d)
        return copy(cross_out.at[at], cross_in.at[at], cross_s.at[d], cross_r.at[at], in_x(at))

    each(NX, lambda d: cross_to(d).start())

    each(NX, lambda d: gram_from(d).wait_recv())
    gram = grams[0]
    for k in range(1, NX):
        gram = gram + grams[k]
    mean_pred = jnp.broadcast_to(gram[TILE : TILE + 1] / ensemble, (TILE, TILE))
    mean_turned = mean_pred.T
    system = (gram[:TILE] - ensemble * mean_turned * mean_pred) * coupled[...] + spread[...]

    inverted = inverse_blocks(system, 0, TILE // PANEL // 2)

    each(NX, lambda d: cross_from(d).wait_recv())
    cross = cross_in[0]
    for k in range(1, NX):
        cross = cross + cross_in[k]
    mean_param = cross[TILE : TILE + 1] / ensemble
    crosses[x] = cross[:TILE] - ensemble * mean_turned * mean_param

    def crosses_to(d):
        return copy(crosses.at[x], crosses.at[x], crosses_s.at[d], crosses_r.at[x], in_x(x_at(d)))

    def crosses_from(d):
        at = x_at(d)
        return copy(crosses.at[at], crosses.at[at], crosses_s.at[d], crosses_r.at[at], in_x(at))

    each(NX, lambda d: crosses_to(d).start())

    inverted = inverse_blocks(inverted, TILE // PANEL // 2, TILE // PANEL)

    each(NX, lambda d: crosses_from(d).wait_recv())
    cross = jnp.concatenate([crosses[k] for k in range(NX)], axis=1)
    gain = dot(inverted, cross, PLAIN, lax.Precision.HIGHEST) / (ensemble - 1)
    high = gain.astype(BF16)
    low = (gain - high.astype(F32)).astype(BF16)
    weights = jnp.concatenate([high, low], axis=1)
    weights = jnp.concatenate([weights, weights], axis=0)

    def share(core):
        left = innov[core].reshape(ny * side, TILE)
        big = left.astype(BF16)
        small = (left - big.astype(F32)).astype(BF16)
        parts = dot(jnp.concatenate([big, small], axis=1), weights, PLAIN)
        return (parts[:, :width] + parts[:, width:]).reshape(ny, side, width)

    def pair_copy(d):
        at = y_at(d)
        return copy(pair_out.at[at], pair_in.at[at], pair_s.at[at], pair_r.at[at], (g, sibling))

    def share_to(d):
        at = y_at(d)
        return copy(share_out.at[at], share_in.at[y], share_s.at[d], share_r.at[y], (g, at * 2 + c))

    def share_from(d):
        at = y_at(d)
        return copy(share_out.at[at], share_in.at[at], share_s.at[d], share_r.at[at], (g, at * 2 + c))

    turns = sorted(range(1, ny), key=lambda d: -min(d, ny - d)) + [0]
    pair_out[...] = share(1 - c).astype(BF16)
    for d in turns:
        pair_copy(d).start()
    mine[...] = share(c)
    for d in turns:
        at = y_at(d)
        pair_copy(d).wait_recv()
        total = mine[at] + pair_in[at].astype(F32)
        if d:
            share_out[at] = total.astype(BF16)
            share_to(d).start()
    for d in turns[:-1]:
        share_from(d).wait_recv()
        total = total + share_in[y_at(d)].astype(F32)
    incr_out[...] = total.reshape(nz, ROWS, width)

    def incr_to(d):
        at = z_at(d)
        return copy(incr_out.at[at], final.at[z], incr_s.at[d], incr_r.at[z], in_z(at))

    def incr_from(d):
        at = z_at(d)
        return copy(incr_out.at[at], final.at[at], incr_s.at[d], incr_r.at[at], in_z(at))

    each(nz, lambda d: incr_to(d).start())
    final[z] = incr_out[z]
    each(nz, lambda d: incr_from(d).wait_recv())
    for k in range(nz):
        at = slice(k * width, (k + 1) * width)
        out[:, at] = members[:, at].astype(F32) + final[k]

    def obs_sent(d):
        rows_to(d).wait_send()

    def y_sent(d):
        slab_to(d).wait_send()
        slab_pass(d).wait_send()
        share_to(d).wait_send()
        pair_copy(d).wait_send()

    def z_sent(d):
        block_to(d).wait_send()
        pert_to(d).wait_send()
        pred_to(d).wait_send()
        incr_to(d).wait_send()

    def x_sent(d):
        gram_to(d).wait_send()
        cross_to(d).wait_send()
        crosses_to(d).wait_send()

    half_copy.wait_send()
    slab_own.wait_send()
    pair_copy(0).wait_send()
    each(no, obs_sent)
    each(ny, y_sent)
    each(nz, z_sent)
    each(NX, x_sent)


def shards(members, alphas, points, labels, noise, observed, perturb):
    nm, no = lax.axis_size("mem"), lax.axis_size("obs")
    nz, ny = nm // NX, no // 2
    coeffs = members.shape[1]
    dims = alphas.shape[0]
    side, width = nz * ROWS, coeffs // nz
    vmem, many = pltpu.VMEM, pltpu.SemaphoreType.DMA
    signal = pltpu.SemaphoreType.REGULAR
    stages = nz // 2 - 1
    return pl.pallas_call(
        lambda *refs: kernel(nm, no, *refs),
        out_shape=jax.ShapeDtypeStruct((ROWS, coeffs), F32),
        in_specs=[pl.BlockSpec(memory_space=pl.ANY)] * 7,
        out_specs=pl.BlockSpec(memory_space=vmem),
        scratch_shapes=[
            vmem((ROWS, coeffs), BF16),
            vmem((dims, coeffs), jnp.int32),
            vmem((dims, 2 * TILE), F32),
            vmem((1, TILE), jnp.int32),
            vmem((1, TILE), F32),
            vmem((1, TILE), F32),
            vmem((2, 2 * ROWS, coeffs // 4), BF16),
            vmem((no, 2 * ROWS, coeffs // 4), BF16),
            vmem((2, no * ROWS, TILE), F32),
            vmem((no * ROWS, TILE), F32),
            vmem((nz, 2 * ROWS, width // 2), BF16),
            vmem((nz, 2 * ROWS, width // 2), BF16),
            vmem((no, side, width), BF16),
            vmem((nz, no * ROWS, TILE), BF16),
            vmem((nz, no * ROWS, TILE), BF16),
            vmem((NX, TILE + ROWS, TILE), F32),
            vmem((2, dims, 3, TILE, TILE), F32),
            vmem((4 * TILE, coeffs // 4), BF16),
            vmem((2, ny, side, TILE), F32),
            vmem((no, side, TILE), F32),
            vmem((NX, TILE + ROWS, SLAB), F32),
            vmem((NX, TILE + ROWS, SLAB), F32),
            vmem((NX, TILE, SLAB), F32),
            vmem((ny, side, width), F32),
            vmem((ny, side, width), BF16),
            vmem((ny, side, width), BF16),
            vmem((ny, side, width), BF16),
            vmem((ny, side, width), BF16),
            vmem((nz, ROWS, width), F32),
            vmem((nz, ROWS, width), F32),
            vmem((TILE, TILE), F32),
            vmem((TILE, TILE), F32),
            signal((stages,)),
            signal((stages,)),
            many((7,)),
            many((no,)),
            many((no,)),
            many,
            many,
            many((nz,)),
            many((nz,)),
            many((no,)),
            many((no,)),
            many((nz,)),
            many((nz,)),
            many((nz,)),
            many((nz,)),
            many((NX,)),
            many((NX,)),
            many((NX,)),
            many((NX,)),
            many((NX,)),
            many((NX,)),
            many((ny,)),
            many((ny,)),
            many((ny,)),
            many((ny,)),
            many((nz,)),
            many((nz,)),
        ],
        compiler_params=pltpu.CompilerParams(
            collective_id=0, has_side_effects=True, vmem_limit_bytes=60 * 1024 * 1024
        ),
    )(members, alphas, points, labels.reshape(1, TILE), noise.reshape(1, TILE), observed.reshape(1, TILE), perturb)


def solution(mesh):
    in_specs = (P(("mem", "obs"), None), P(), P(), P("obs"), P("obs"), P("obs"), P("mem", "obs"))
    out_specs = P(("mem", "obs"), None)
    return jax.shard_map(shards, mesh=mesh, in_specs=in_specs, out_specs=out_specs, check_vma=False)
```

```python
import math

import jax
import jax.numpy as jnp
from jax import lax
from jax.experimental import pallas as pl
from jax.experimental.pallas import tpu as pltpu
from jax.sharding import PartitionSpec as P

ROWS = 8
TILE = 128
SLAB = 128
PANEL = 8
CHUNK = 256
NX = 4
F32 = jnp.float32
BF16 = jnp.bfloat16
FIRST = (((0,), (0,)), ((), ()))
LAST = (((1,), (1,)), ((), ()))
PLAIN = (((1,), (0,)), ((), ()))


def dot(left, right, dims, precision=None):
    return lax.dot_general(left, right, dims, precision=precision, preferred_element_type=F32)


def inverse_blocks(matrix, first, last):
    size = matrix.shape[0]
    row = lax.broadcasted_iota(jnp.int32, (PANEL, size), 0)
    lane = lax.broadcasted_iota(jnp.int32, (PANEL, size), 1)
    rest_lane = lax.broadcasted_iota(jnp.int32, (size - PANEL, size), 1)
    unit = jnp.where(lane == row, 1.0, 0.0).astype(F32)

    def block(_, full):
        top, rest = full[:PANEL], full[PANEL:]
        column = [jnp.broadcast_to(top[:, j : j + 1], (PANEL, size)) for j in range(PANEL)]
        panel = jnp.where(lane < PANEL, unit, top)
        for p in range(PANEL):
            scale = 1.0 / column[p][p : p + 1]
            pivot = panel[p : p + 1] * scale
            panel = jnp.where(row == p, pivot, panel - column[p] * pivot)
            for j in range(p + 1, PANEL):
                entry = column[j][p : p + 1] * scale
                column[j] = jnp.where(row == p, entry, column[j] - column[p] * entry)
        update = jnp.where(rest_lane < PANEL, 0.0, rest)
        for j in range(PANEL):
            update = update - rest[:, j : j + 1] * panel[j : j + 1]
        return pltpu.roll(jnp.concatenate([update, panel], axis=0), size - PANEL, 1)

    return lax.fori_loop(first, last, block, matrix)


def places(rows):
    shape = (rows, TILE)
    return lax.broadcasted_iota(jnp.int32, shape, 0), lax.broadcasted_iota(jnp.int32, shape, 1)


def folded(square):
    edge = TILE // 2
    row, lane = places(edge)
    return jnp.where(lane >= row, square[:edge], pltpu.roll(square[edge:], edge, 1))


def diagonal_row(square):
    row, lane = places(TILE)
    kept = jnp.sum(jnp.where(row == lane, square, 0.0), axis=0, keepdims=True)
    return jnp.broadcast_to(kept, (ROWS, TILE))


def unfolded(half, kept):
    edge = TILE // 2
    row, lane = places(TILE)
    whole = jnp.concatenate([half, pltpu.roll(half, edge, 1)], axis=0)
    direct = jnp.where(row < edge, lane - row, jnp.where(lane >= edge, row - lane - 1, -1)) >= 0
    square = jnp.where(direct, whole, whole.T)
    return jnp.where((row == lane) & (row >= edge), jnp.broadcast_to(kept[:1], (TILE, TILE)), square)


def kernel(
    nm,
    no,
    members_hbm,
    alphas_hbm,
    points_hbm,
    labels_hbm,
    noise_hbm,
    observed_hbm,
    perturb_hbm,
    out,
    members,
    alphas,
    points,
    labels,
    noise,
    observed,
    rows_out,
    rows_in,
    halves,
    half_in,
    blocks_out,
    blocks_in,
    slabs,
    preds,
    perts,
    grams,
    table,
    basis,
    innov,
    prior,
    cross_out,
    cross_in,
    crosses,
    pair_out,
    pair_in,
    share_out,
    share_in,
    incr_out,
    final,
    coupled,
    spread,
    ready,
    local_s,
    rows_s,
    rows_r,
    half_s,
    half_r,
    blocks_s,
    blocks_r,
    slabs_s,
    slabs_r,
    preds_s,
    preds_r,
    perts_s,
    perts_r,
    grams_s,
    grams_r,
    cross_s,
    cross_r,
    crosses_s,
    crosses_r,
    pair_s,
    pair_r,
    share_s,
    share_r,
    incr_s,
    incr_r,
):
    g, o = lax.axis_index("mem"), lax.axis_index("obs")
    z, x = lax.div(g, NX), lax.rem(g, NX)
    y, c = lax.div(o, 2), lax.rem(o, 2)
    nz, ny = nm // NX, no // 2
    coeffs = members.shape[1]
    half = coeffs // 2
    quarter = half // 2
    width = coeffs // nz
    chunk = min(CHUNK, quarter)
    ensemble = nm * no * ROWS
    line = nz * no * ROWS
    side = nz * ROWS
    mesh = pl.DeviceIdType.MESH

    def obs_at(d):
        return lax.rem(o + d, no)

    def z_at(d):
        return lax.rem(z + d, nz)

    def x_at(d):
        return lax.rem(x + d, NX)

    def y_at(d):
        return lax.rem(y + d, ny)

    def in_z(at):
        return (at * NX + x, o)

    def in_x(at):
        return (z * NX + at, o)

    sibling = y * 2 + 1 - c

    def copy(src, dst, send, recv, to):
        return pltpu.make_async_remote_copy(
            src_ref=src, dst_ref=dst, send_sem=send, recv_sem=recv, device_id=to, device_id_type=mesh
        )

    def tell(semaphore, to):
        pl.semaphore_signal(semaphore, inc=1, device_id=to, device_id_type=mesh)

    def each(count, act):
        def step(d, carry):
            act(d)
            return carry

        lax.fori_loop(1, count, step, 0)

    far = sorted(range(1, nz), key=lambda d: -min(d, nz - d))

    turns_z = far + [0]
    turns = sorted(range(1, ny), key=lambda d: -min(d, ny - d)) + [0]
    fore = side // 2

    fetch = [
        pltpu.make_async_copy(src, dst, local_s.at[k])
        for k, (src, dst) in enumerate(
            (
                (members_hbm, members),
                (points_hbm.at[:, pl.ds(pl.multiple_of(y * 2 * TILE, 2 * TILE), 2 * TILE)], points),
                (labels_hbm, labels),
                (noise_hbm, noise),
                (observed_hbm, observed),
                (perturb_hbm, perts.at[z]),
                (alphas_hbm, alphas),
            )
        )
    ]
    for f in fetch:
        f.start()

    barrier = pltpu.get_barrier_semaphore()
    reach = range(1, nz // 4 + 1)
    near = [in_z(z_at(s * k % nz)) for k in reach for s in (1, -1)]
    each(no, lambda d: tell(barrier, (g, obs_at(d))))
    each(NX, lambda d: tell(barrier, in_x(x_at(d))))
    for to in near:
        tell(barrier, to)

    fetch[0].wait()
    own = members[...].astype(F32)
    for h in range(2):
        part = own[:, h * half : (h + 1) * half]
        rows_out[h] = jnp.concatenate([part[:, :quarter], part[:, quarter:]], axis=0).astype(BF16)
    rows_in[o] = rows_out[c]
    for k in range(nz):
        part = own[:, k * width : (k + 1) * width]
        blocks_out[k] = jnp.concatenate([part[:, : width // 2], part[:, width // 2 :]], axis=0).astype(BF16)
    blocks_in[z] = blocks_out[z]

    pl.semaphore_wait(barrier, no - 1 + NX - 1 + len(near))

    def rows_to(d):
        to = obs_at(d)
        return copy(rows_out.at[lax.rem(to, 2)], rows_in.at[o], rows_s.at[d], rows_r.at[o], (g, to))

    def rows_from(d):
        at = obs_at(d)
        return copy(rows_out.at[c], rows_in.at[at], rows_s.at[d], rows_r.at[at], (g, at))

    for d in sorted(range(1, no), key=lambda d: -min(d, no - d)):
        rows_to(d).start()
    for to in near[-2:]:
        tell(ready, to)

    fetch[1].wait()

    def tabulate(t):
        at = points[:, t * TILE : (t + 1) * TILE]
        turned = jnp.concatenate([at, jnp.zeros((TILE - at.shape[0], TILE), F32)], axis=0).T
        for d in range(at.shape[0]):
            value = jnp.broadcast_to(turned[:, d : d + 1], (TILE, TILE))
            second = value * value - 1.0
            third = value * second - 2.0 * value
            table[t, d, 0] = value
            table[t, d, 1] = second * (1.0 / math.sqrt(2.0))
            table[t, d, 2] = third * (1.0 / math.sqrt(6.0))

    tabulate(0)
    tabulate(1)

    for f in fetch[2:]:
        f.wait()
    label = jnp.broadcast_to(labels[...].astype(F32), (TILE, TILE))
    diagonal = lax.broadcasted_iota(jnp.int32, (TILE, TILE), 0) == lax.broadcasted_iota(jnp.int32, (TILE, TILE), 1)
    coupled[...] = jnp.where(label == label.T, 1.0 / (ensemble - 1), 0.0).astype(F32)
    spread[...] = jnp.where(diagonal, jnp.broadcast_to(noise[...], (TILE, TILE)), 0.0)

    def basis_part(first_step, last_step):
        def step(n, carry):
            per = quarter // chunk
            q, t, k = lax.div(n, 2 * per), lax.rem(lax.div(n, per), 2), lax.rem(n, per)
            first = pl.multiple_of(k * chunk, chunk)
            degree = alphas[:, pl.ds(pl.multiple_of(c * half + q * quarter + first, chunk), chunk)]
            product = None
            for d in range(degree.shape[0]):
                odd = (degree[d : d + 1] & 1) == 1
                high = degree[d : d + 1] >= 2
                one, two, three = (jnp.concatenate([table[t, d, p]] * (chunk // TILE), axis=1) for p in range(3))
                value = jnp.where(high, jnp.where(odd, three, two), jnp.where(odd, one, 1.0))
                product = value if product is None else product * value
            place = pl.multiple_of((q * 2 + t) * TILE, TILE)
            basis[pl.ds(place, TILE), pl.ds(first, chunk)] = product.astype(BF16)
            return carry

        lax.fori_loop(first_step, last_step, step, 0)

    steps = 4 * (quarter // chunk)
    basis_part(0, steps // 8)
    pl.semaphore_wait(ready, 2)

    def block_to(d):
        return copy(blocks_out.at[z_at(d)], blocks_in.at[z], blocks_s.at[d], blocks_r.at[z], in_z(z_at(d)))

    def block_from(d):
        at = z_at(d)
        return copy(blocks_out.at[at], blocks_in.at[at], blocks_s.at[d], blocks_r.at[at], in_z(at))

    def pert_to(d):
        return copy(perts.at[z], perts.at[z], perts_s.at[d], perts_r.at[z], in_z(z_at(d)))

    def pert_from(d):
        at = z_at(d)
        return copy(perts.at[at], perts.at[at], perts_s.at[d], perts_r.at[at], in_z(at))

    for d in far:
        block_to(d).start()
    basis_part(steps // 8, steps)

    each(no, lambda d: rows_from(d).wait_recv())
    both = dot(rows_in[...].reshape(no * 2 * ROWS, quarter), basis[...], LAST)
    both = both.reshape(no, 2, ROWS, 4 * TILE)
    part = (both[:, 0, :, : 2 * TILE] + both[:, 1, :, 2 * TILE :]).reshape(no * ROWS, 2 * TILE)
    for t in range(2):
        halves[t] = part[:, t * TILE : (t + 1) * TILE]
    half_copy = copy(halves.at[1 - c], half_in, half_s, half_r, (g, sibling))
    half_copy.start()
    half_copy.wait_recv()
    preds[z] = (halves[c] + half_in[...]).astype(BF16)

    def pred_to(d):
        return copy(preds.at[z], preds.at[z], preds_s.at[d], preds_r.at[z], in_z(z_at(d)))

    def pred_from(d):
        at = z_at(d)
        return copy(preds.at[at], preds.at[at], preds_s.at[d], preds_r.at[at], in_z(at))

    for d in far:
        pred_to(d).start()

    each(nz, lambda d: block_from(d).wait_recv())
    block = blocks_in[...].astype(F32)
    block = jnp.concatenate([block[:, :ROWS], block[:, ROWS:]], axis=2)
    slabs[o] = block.reshape(side, width).astype(BF16)

    def slab_to(d):
        return copy(slabs.at[o], slabs.at[o], slabs_s.at[d], slabs_r.at[o], (g, y_at(d) * 2 + c))

    def slab_from(at, to):
        return copy(slabs.at[at], slabs.at[at], slabs_s.at[0], slabs_r.at[at], (g, to))

    def slab_pass(d):
        at = y_at(d) * 2 + c
        return copy(slabs.at[at], slabs.at[at], slabs_s.at[ny + d], slabs_r.at[at], (g, sibling))

    slab_own = copy(slabs.at[o], slabs.at[o], slabs_s.at[0], slabs_r.at[o], (g, sibling))
    each(ny, lambda d: slab_to(d).start())
    slab_own.start()

    def pass_on(d):
        at = y_at(d) * 2 + c
        slab_from(at, at).wait_recv()
        slab_pass(d).start()

    each(ny, pass_on)

    each(nz, lambda d: pred_from(d).wait_recv())
    flat = preds[...].reshape(line, TILE)
    ones = jnp.ones((2 * ROWS, line), BF16)
    gram = dot(flat, flat, FIRST)
    grams[x] = jnp.concatenate([folded(gram), dot(ones, flat, PLAIN)[:ROWS], diagonal_row(gram)], axis=0)

    def gram_to(d):
        return copy(grams.at[x], grams.at[x], grams_s.at[d], grams_r.at[x], in_x(x_at(d)))

    def gram_from(d):
        at = x_at(d)
        return copy(grams.at[at], grams.at[at], grams_s.at[d], grams_r.at[at], in_x(at))

    each(NX, lambda d: gram_to(d).start())
    for d in far:
        pert_to(d).start()

    for t in range(nz):
        value = preds[t].astype(F32)
        for k in range(no):
            prior[k, t * ROWS : (t + 1) * ROWS, :] = value[k * ROWS : (k + 1) * ROWS]
    ordered = prior[...].reshape(line, TILE).astype(BF16)

    slab_from(sibling, sibling).wait_recv()
    each(ny, lambda d: slab_from(y_at(d) * 2 + 1 - c, sibling).wait_recv())
    slab = slabs[...].reshape(line, width)
    raw = dot(ordered, slab, FIRST)
    total = dot(ones, slab, PLAIN)[:ROWS]
    for k in range(NX):
        cross_out[k, :TILE] = raw[:, k * SLAB : (k + 1) * SLAB]
        cross_out[k, TILE:] = total[:, k * SLAB : (k + 1) * SLAB]
    cross_in[x] = cross_out[x]

    def cross_to(d):
        at = x_at(d)
        return copy(cross_out.at[at], cross_in.at[x], cross_s.at[d], cross_r.at[x], in_x(at))

    def cross_from(d):
        at = x_at(d)
        return copy(cross_out.at[at], cross_in.at[at], cross_s.at[d], cross_r.at[at], in_x(at))

    each(NX, lambda d: cross_to(d).start())

    each(NX, lambda d: gram_from(d).wait_recv())
    gram = grams[0]
    for k in range(1, NX):
        gram = gram + grams[k]
    mean_pred = jnp.broadcast_to(gram[TILE // 2 : TILE // 2 + 1] / ensemble, (TILE, TILE))
    mean_turned = mean_pred.T
    gram = unfolded(gram[: TILE // 2], gram[TILE // 2 + ROWS :])
    system = (gram - ensemble * mean_turned * mean_pred) * coupled[...] + spread[...]

    inverted = inverse_blocks(system, 0, TILE // PANEL // 2)

    each(NX, lambda d: cross_from(d).wait_recv())
    cross = cross_in[0]
    for k in range(1, NX):
        cross = cross + cross_in[k]
    mean_param = cross[TILE : TILE + 1] / ensemble
    crosses[x] = cross[:TILE] - ensemble * mean_turned * mean_param

    def crosses_to(d):
        return copy(crosses.at[x], crosses.at[x], crosses_s.at[d], crosses_r.at[x], in_x(x_at(d)))

    def crosses_from(d):
        at = x_at(d)
        return copy(crosses.at[at], crosses.at[at], crosses_s.at[d], crosses_r.at[at], in_x(at))

    each(NX, lambda d: crosses_to(d).start())

    each(nz, lambda d: pert_from(d).wait_recv())
    noise_root = jnp.sqrt(noise[...])
    for t, d in enumerate(turns_z):
        at = z_at(d)
        left = observed[...] + noise_root * perts[at].astype(F32) - preds[at].astype(F32)
        for k in range(no):
            innov[k % 2, k // 2, t * ROWS : (t + 1) * ROWS, :] = left[k * ROWS : (k + 1) * ROWS]

    inverted = inverse_blocks(inverted, TILE // PANEL // 2, TILE // PANEL)

    each(NX, lambda d: crosses_from(d).wait_recv())
    cross = jnp.concatenate([crosses[k] for k in range(NX)], axis=1)
    gain = dot(inverted, cross, PLAIN, lax.Precision.HIGHEST) / (ensemble - 1)
    high = gain.astype(BF16)
    low = (gain - high.astype(F32)).astype(BF16)
    weights = jnp.concatenate([high, low], axis=1)
    weights = jnp.concatenate([weights, weights], axis=0)

    def share(core, d):
        left = innov[core, y_at(d)]
        big = left.astype(BF16)
        small = (left - big.astype(F32)).astype(BF16)
        parts = dot(jnp.concatenate([big, small], axis=1), weights, PLAIN)
        return parts[:, :width] + parts[:, width:]

    def pair_copy(d):
        return copy(pair_out.at[d], pair_in.at[d], pair_s.at[d], pair_r.at[d], (g, sibling))

    def share_to(d, h):
        span = pl.ds(h * fore, fore)
        to = (g, y_at(d) * 2 + c)
        return copy(share_out.at[d, span], share_in.at[y, span], share_s.at[d, h], share_r.at[y, h], to)

    def share_from(d, h):
        at = y_at(d)
        span = pl.ds(h * fore, fore)
        return copy(share_out.at[d, span], share_in.at[at, span], share_s.at[d, h], share_r.at[at, h], (g, at * 2 + c))

    def incr_to(t):
        at = z_at(turns_z[t])
        return copy(incr_out.at[t], final.at[z], incr_s.at[t], incr_r.at[z], in_z(at))

    def incr_from(d):
        at = z_at(d)
        return copy(incr_out.at[0], final.at[at], incr_s.at[0], incr_r.at[at], in_z(at))

    for d in turns:
        pair_out[d] = share(1 - c, d).astype(BF16)
        pair_copy(d).start()
    for d in turns:
        total = share(c, d)
        pair_copy(d).wait_recv()
        total = total + pair_in[d].astype(F32)
        if d:
            share_out[d] = total.astype(BF16)
            share_to(d, 0).start()
    for d in turns[:-1]:
        share_to(d, 1).start()
    for h in range(2):
        part = total[h * fore : (h + 1) * fore]
        for d in turns[:-1]:
            share_from(d, h).wait_recv()
            part = part + share_in[y_at(d), h * fore : (h + 1) * fore].astype(F32)
        for t in range(h * nz // 2, (h + 1) * nz // 2):
            first = t * ROWS - h * fore
            incr_out[t] = part[first : first + ROWS]
            if t < nz - 1:
                incr_to(t).start()
    final[z] = incr_out[nz - 1]
    each(nz, lambda d: incr_from(d).wait_recv())
    for k in range(nz):
        at = slice(k * width, (k + 1) * width)
        out[:, at] = members[:, at].astype(F32) + final[k]

    def y_sent(d):
        slab_to(d).wait_send()
        slab_pass(d).wait_send()
        share_to(d, 0).wait_send()
        share_to(d, 1).wait_send()
        pair_copy(d).wait_send()

    def z_sent(d):
        block_to(d).wait_send()
        pert_to(d).wait_send()
        pred_to(d).wait_send()

    def x_sent(d):
        gram_to(d).wait_send()
        cross_to(d).wait_send()
        crosses_to(d).wait_send()

    each(no, lambda d: rows_to(d).wait_send())
    half_copy.wait_send()
    slab_own.wait_send()
    pair_copy(0).wait_send()
    each(ny, y_sent)
    each(nz, z_sent)
    for t in range(nz - 1):
        incr_to(t).wait_send()
    each(NX, x_sent)


def shards(members, alphas, points, labels, noise, observed, perturb):
    nm, no = lax.axis_size("mem"), lax.axis_size("obs")
    nz, ny = nm // NX, no // 2
    coeffs = members.shape[1]
    dims = alphas.shape[0]
    side, width = nz * ROWS, coeffs // nz
    vmem, many = pltpu.VMEM, pltpu.SemaphoreType.DMA
    signal = pltpu.SemaphoreType.REGULAR
    return pl.pallas_call(
        lambda *refs: kernel(nm, no, *refs),
        out_shape=jax.ShapeDtypeStruct((ROWS, coeffs), F32),
        in_specs=[pl.BlockSpec(memory_space=pl.ANY)] * 7,
        out_specs=pl.BlockSpec(memory_space=vmem),
        scratch_shapes=[
            vmem((ROWS, coeffs), BF16),
            vmem((dims, coeffs), jnp.int32),
            vmem((dims, 2 * TILE), F32),
            vmem((1, TILE), jnp.int32),
            vmem((1, TILE), F32),
            vmem((1, TILE), F32),
            vmem((2, 2 * ROWS, coeffs // 4), BF16),
            vmem((no, 2 * ROWS, coeffs // 4), BF16),
            vmem((2, no * ROWS, TILE), F32),
            vmem((no * ROWS, TILE), F32),
            vmem((nz, 2 * ROWS, width // 2), BF16),
            vmem((nz, 2 * ROWS, width // 2), BF16),
            vmem((no, side, width), BF16),
            vmem((nz, no * ROWS, TILE), BF16),
            vmem((nz, no * ROWS, TILE), BF16),
            vmem((NX, TILE // 2 + 2 * ROWS, TILE), F32),
            vmem((2, dims, 3, TILE, TILE), F32),
            vmem((4 * TILE, coeffs // 4), BF16),
            vmem((2, ny, side, TILE), F32),
            vmem((no, side, TILE), F32),
            vmem((NX, TILE + ROWS, SLAB), F32),
            vmem((NX, TILE + ROWS, SLAB), F32),
            vmem((NX, TILE, SLAB), F32),
            vmem((ny, side, width), BF16),
            vmem((ny, side, width), BF16),
            vmem((ny, side, width), BF16),
            vmem((ny, side, width), BF16),
            vmem((nz, ROWS, width), F32),
            vmem((nz, ROWS, width), F32),
            vmem((TILE, TILE), F32),
            vmem((TILE, TILE), F32),
            signal,
            many((7,)),
            many((no,)),
            many((no,)),
            many,
            many,
            many((nz,)),
            many((nz,)),
            many((no,)),
            many((no,)),
            many((nz,)),
            many((nz,)),
            many((nz,)),
            many((nz,)),
            many((NX,)),
            many((NX,)),
            many((NX,)),
            many((NX,)),
            many((NX,)),
            many((NX,)),
            many((ny,)),
            many((ny,)),
            many((ny, 2)),
            many((ny, 2)),
            many((nz,)),
            many((nz,)),
        ],
        compiler_params=pltpu.CompilerParams(
            collective_id=0, has_side_effects=True, vmem_limit_bytes=60 * 1024 * 1024
        ),
    )(members, alphas, points, labels.reshape(1, TILE), noise.reshape(1, TILE), observed.reshape(1, TILE), perturb)


def solution(mesh):
    in_specs = (P(("mem", "obs"), None), P(), P(), P("obs"), P("obs"), P("obs"), P("mem", "obs"))
    out_specs = P(("mem", "obs"), None)
    return jax.shard_map(shards, mesh=mesh, in_specs=in_specs, out_specs=out_specs, check_vma=False)
```

```python
import math

import jax
import jax.numpy as jnp
from jax import lax
from jax.experimental import pallas as pl
from jax.experimental.pallas import tpu as pltpu
from jax.sharding import PartitionSpec as P

ROWS = 8
TILE = 128
SLAB = 128
PANEL = 8
CHUNK = 256
NX = 4
F32 = jnp.float32
BF16 = jnp.bfloat16
FIRST = (((0,), (0,)), ((), ()))
LAST = (((1,), (1,)), ((), ()))
PLAIN = (((1,), (0,)), ((), ()))


def dot(left, right, dims, precision=None):
    return lax.dot_general(left, right, dims, precision=precision, preferred_element_type=F32)


def inverse_blocks(matrix, first, last):
    size = matrix.shape[0]
    row = lax.broadcasted_iota(jnp.int32, (PANEL, size), 0)
    lane = lax.broadcasted_iota(jnp.int32, (PANEL, size), 1)
    rest_lane = lax.broadcasted_iota(jnp.int32, (size - PANEL, size), 1)
    unit = jnp.where(lane == row, 1.0, 0.0).astype(F32)

    def block(_, full):
        top, rest = full[:PANEL], full[PANEL:]
        column = [jnp.broadcast_to(top[:, j : j + 1], (PANEL, size)) for j in range(PANEL)]
        panel = jnp.where(lane < PANEL, unit, top)
        for p in range(PANEL):
            scale = 1.0 / column[p][p : p + 1]
            pivot = panel[p : p + 1] * scale
            panel = jnp.where(row == p, pivot, panel - column[p] * pivot)
            for j in range(p + 1, PANEL):
                entry = column[j][p : p + 1] * scale
                column[j] = jnp.where(row == p, entry, column[j] - column[p] * entry)
        update = jnp.where(rest_lane < PANEL, 0.0, rest)
        for j in range(PANEL):
            update = update - rest[:, j : j + 1] * panel[j : j + 1]
        return pltpu.roll(jnp.concatenate([update, panel], axis=0), size - PANEL, 1)

    return lax.fori_loop(first, last, block, matrix)


def places(rows):
    shape = (rows, TILE)
    return lax.broadcasted_iota(jnp.int32, shape, 0), lax.broadcasted_iota(jnp.int32, shape, 1)


def folded(square):
    edge = TILE // 2
    row, lane = places(edge)
    return jnp.where(lane >= row, square[:edge], pltpu.roll(square[edge:], edge, 1))


def diagonal_row(square):
    row, lane = places(TILE)
    kept = jnp.sum(jnp.where(row == lane, square, 0.0), axis=0, keepdims=True)
    return jnp.broadcast_to(kept, (ROWS, TILE))


def unfolded(half, kept):
    edge = TILE // 2
    row, lane = places(TILE)
    whole = jnp.concatenate([half, pltpu.roll(half, edge, 1)], axis=0)
    direct = jnp.where(row < edge, lane - row, jnp.where(lane >= edge, row - lane - 1, -1)) >= 0
    square = jnp.where(direct, whole, whole.T)
    return jnp.where((row == lane) & (row >= edge), jnp.broadcast_to(kept[:1], (TILE, TILE)), square)


def kernel(
    nm,
    no,
    members_hbm,
    alphas_hbm,
    points_hbm,
    labels_hbm,
    noise_hbm,
    observed_hbm,
    perturb_hbm,
    out,
    members,
    alphas,
    points,
    labels,
    noise,
    observed,
    rows_out,
    rows_in,
    halves,
    half_in,
    blocks_out,
    blocks_in,
    slabs,
    preds,
    perts,
    grams,
    table,
    basis,
    innov,
    prior,
    cross_out,
    cross_in,
    crosses,
    pair_out,
    pair_in,
    share_out,
    share_in,
    incr_out,
    final,
    coupled,
    spread,
    ready,
    local_s,
    rows_s,
    rows_r,
    half_s,
    half_r,
    blocks_s,
    blocks_r,
    slabs_s,
    slabs_r,
    preds_s,
    preds_r,
    perts_s,
    perts_r,
    grams_s,
    grams_r,
    cross_s,
    cross_r,
    crosses_s,
    crosses_r,
    pair_s,
    pair_r,
    share_s,
    share_r,
    incr_s,
    incr_r,
):
    g, o = lax.axis_index("mem"), lax.axis_index("obs")
    z, x = lax.div(g, NX), lax.rem(g, NX)
    y, c = lax.div(o, 2), lax.rem(o, 2)
    nz, ny = nm // NX, no // 2
    coeffs = members.shape[1]
    half = coeffs // 2
    quarter = half // 2
    width = coeffs // nz
    chunk = min(CHUNK, quarter)
    ensemble = nm * no * ROWS
    line = nz * no * ROWS
    side = nz * ROWS
    mesh = pl.DeviceIdType.MESH

    def obs_at(d):
        return lax.rem(o + d, no)

    def z_at(d):
        return lax.rem(z + d, nz)

    def x_at(d):
        return lax.rem(x + d, NX)

    def y_at(d):
        return lax.rem(y + d, ny)

    def in_z(at):
        return (at * NX + x, o)

    def in_x(at):
        return (z * NX + at, o)

    sibling = y * 2 + 1 - c

    def copy(src, dst, send, recv, to):
        return pltpu.make_async_remote_copy(
            src_ref=src, dst_ref=dst, send_sem=send, recv_sem=recv, device_id=to, device_id_type=mesh
        )

    def tell(semaphore, to):
        pl.semaphore_signal(semaphore, inc=1, device_id=to, device_id_type=mesh)

    def each(count, act):
        def step(d, carry):
            act(d)
            return carry

        lax.fori_loop(1, count, step, 0)

    far = sorted(range(1, nz), key=lambda d: -min(d, nz - d))

    turns_z = far + [0]
    turns = sorted(range(1, ny), key=lambda d: -min(d, ny - d)) + [0]
    fore = side // 2

    fetch = [
        pltpu.make_async_copy(src, dst, local_s.at[k])
        for k, (src, dst) in enumerate(
            (
                (members_hbm, members),
                (points_hbm.at[:, pl.ds(pl.multiple_of(y * 2 * TILE, 2 * TILE), 2 * TILE)], points),
                (labels_hbm, labels),
                (noise_hbm, noise),
                (observed_hbm, observed),
                (perturb_hbm, perts.at[z]),
                (alphas_hbm, alphas),
            )
        )
    ]
    for f in fetch:
        f.start()

    barrier = pltpu.get_barrier_semaphore()
    reach = range(1, nz // 4 + 1)
    near = [in_z(z_at(s * k % nz)) for k in reach for s in (1, -1)]
    each(no, lambda d: tell(barrier, (g, obs_at(d))))
    each(NX, lambda d: tell(barrier, in_x(x_at(d))))
    for to in near:
        tell(barrier, to)

    fetch[0].wait()
    own = members[...].astype(F32)
    for h in range(2):
        part = own[:, h * half : (h + 1) * half]
        rows_out[h] = jnp.concatenate([part[:, :quarter], part[:, quarter:]], axis=0).astype(BF16)
    rows_in[o] = rows_out[c]
    for k in range(nz):
        part = own[:, k * width : (k + 1) * width]
        blocks_out[k] = jnp.concatenate([part[:, : width // 2], part[:, width // 2 :]], axis=0).astype(BF16)
    blocks_in[z] = blocks_out[z]

    pl.semaphore_wait(barrier, no - 1 + NX - 1 + len(near))

    def rows_to(d):
        to = obs_at(d)
        return copy(rows_out.at[lax.rem(to, 2)], rows_in.at[o], rows_s.at[d], rows_r.at[o], (g, to))

    def rows_from(d):
        at = obs_at(d)
        return copy(rows_out.at[c], rows_in.at[at], rows_s.at[d], rows_r.at[at], (g, at))

    for d in sorted(range(1, no), key=lambda d: -min(d, no - d)):
        rows_to(d).start()
    for to in near[-2:]:
        tell(ready, to)

    fetch[1].wait()

    def tabulate(t):
        at = points[:, t * TILE : (t + 1) * TILE]
        turned = jnp.concatenate([at, jnp.zeros((TILE - at.shape[0], TILE), F32)], axis=0).T
        for d in range(at.shape[0]):
            value = jnp.broadcast_to(turned[:, d : d + 1], (TILE, TILE))
            second = value * value - 1.0
            third = value * second - 2.0 * value
            table[t, d, 0] = value
            table[t, d, 1] = second * (1.0 / math.sqrt(2.0))
            table[t, d, 2] = third * (1.0 / math.sqrt(6.0))

    tabulate(0)
    tabulate(1)

    for f in fetch[2:]:
        f.wait()
    label = jnp.broadcast_to(labels[...].astype(F32), (TILE, TILE))
    diagonal = lax.broadcasted_iota(jnp.int32, (TILE, TILE), 0) == lax.broadcasted_iota(jnp.int32, (TILE, TILE), 1)
    coupled[...] = jnp.where(label == label.T, 1.0 / (ensemble - 1), 0.0).astype(F32)
    spread[...] = jnp.where(diagonal, jnp.broadcast_to(noise[...], (TILE, TILE)), 0.0)

    def basis_part(first_step, last_step):
        def step(n, carry):
            per = quarter // chunk
            q, t, k = lax.div(n, 2 * per), lax.rem(lax.div(n, per), 2), lax.rem(n, per)
            first = pl.multiple_of(k * chunk, chunk)
            degree = alphas[:, pl.ds(pl.multiple_of(c * half + q * quarter + first, chunk), chunk)]
            product = None
            for d in range(degree.shape[0]):
                odd = (degree[d : d + 1] & 1) == 1
                high = degree[d : d + 1] >= 2
                one, two, three = (jnp.concatenate([table[t, d, p]] * (chunk // TILE), axis=1) for p in range(3))
                value = jnp.where(high, jnp.where(odd, three, two), jnp.where(odd, one, 1.0))
                product = value if product is None else product * value
            place = pl.multiple_of((q * 2 + t) * TILE, TILE)
            basis[pl.ds(place, TILE), pl.ds(first, chunk)] = product.astype(BF16)
            return carry

        lax.fori_loop(first_step, last_step, step, 0)

    steps = 4 * (quarter // chunk)
    basis_part(0, steps // 8)
    pl.semaphore_wait(ready, 2)

    def block_to(d):
        return copy(blocks_out.at[z_at(d)], blocks_in.at[z], blocks_s.at[d], blocks_r.at[z], in_z(z_at(d)))

    def block_from(d):
        at = z_at(d)
        return copy(blocks_out.at[at], blocks_in.at[at], blocks_s.at[d], blocks_r.at[at], in_z(at))

    def pert_to(d):
        return copy(perts.at[z], perts.at[z], perts_s.at[d], perts_r.at[z], in_z(z_at(d)))

    def pert_from(d):
        at = z_at(d)
        return copy(perts.at[at], perts.at[at], perts_s.at[d], perts_r.at[at], in_z(at))

    for d in far:
        block_to(d).start()
    basis_part(steps // 8, steps)

    each(no, lambda d: rows_from(d).wait_recv())
    both = dot(rows_in[...].reshape(no * 2 * ROWS, quarter), basis[...], LAST)
    both = both.reshape(no, 2, ROWS, 4 * TILE)
    part = (both[:, 0, :, : 2 * TILE] + both[:, 1, :, 2 * TILE :]).reshape(no * ROWS, 2 * TILE)
    for t in range(2):
        halves[t] = part[:, t * TILE : (t + 1) * TILE]
    half_copy = copy(halves.at[1 - c], half_in, half_s, half_r, (g, sibling))
    half_copy.start()
    half_copy.wait_recv()
    preds[z] = (halves[c] + half_in[...]).astype(BF16)

    def pred_to(d):
        return copy(preds.at[z], preds.at[z], preds_s.at[d], preds_r.at[z], in_z(z_at(d)))

    def pred_from(d):
        at = z_at(d)
        return copy(preds.at[at], preds.at[at], preds_s.at[d], preds_r.at[at], in_z(at))

    for d in far:
        pred_to(d).start()

    each(nz, lambda d: block_from(d).wait_recv())
    block = blocks_in[...].astype(F32)
    block = jnp.concatenate([block[:, :ROWS], block[:, ROWS:]], axis=2)
    slabs[o] = block.reshape(side, width).astype(BF16)

    def slab_to(d):
        return copy(slabs.at[o], slabs.at[o], slabs_s.at[d], slabs_r.at[o], (g, y_at(d) * 2 + c))

    def slab_from(at, to):
        return copy(slabs.at[at], slabs.at[at], slabs_s.at[0], slabs_r.at[at], (g, to))

    def slab_pass(d):
        at = y_at(d) * 2 + c
        return copy(slabs.at[at], slabs.at[at], slabs_s.at[ny + d], slabs_r.at[at], (g, sibling))

    slab_own = copy(slabs.at[o], slabs.at[o], slabs_s.at[0], slabs_r.at[o], (g, sibling))
    each(ny, lambda d: slab_to(d).start())
    slab_own.start()

    def pass_on(d):
        at = y_at(d) * 2 + c
        slab_from(at, at).wait_recv()
        slab_pass(d).start()

    each(ny, pass_on)

    each(nz, lambda d: pred_from(d).wait_recv())
    flat = preds[...].reshape(line, TILE)
    ones = jnp.ones((2 * ROWS, line), BF16)
    gram = dot(flat, flat, FIRST)
    grams[x] = jnp.concatenate([folded(gram), dot(ones, flat, PLAIN)[:ROWS], diagonal_row(gram)], axis=0)

    def gram_to(d):
        return copy(grams.at[x], grams.at[x], grams_s.at[d], grams_r.at[x], in_x(x_at(d)))

    def gram_from(d):
        at = x_at(d)
        return copy(grams.at[at], grams.at[at], grams_s.at[d], grams_r.at[at], in_x(at))

    each(NX, lambda d: gram_to(d).start())
    for d in far:
        pert_to(d).start()

    for t in range(nz):
        value = preds[t].astype(F32)
        for k in range(no):
            prior[k, t * ROWS : (t + 1) * ROWS, :] = value[k * ROWS : (k + 1) * ROWS]
    ordered = prior[...].reshape(line, TILE).astype(BF16)

    slab_from(sibling, sibling).wait_recv()
    each(ny, lambda d: slab_from(y_at(d) * 2 + 1 - c, sibling).wait_recv())
    slab = slabs[...].reshape(line, width)
    raw = dot(ordered, slab, FIRST)
    total = dot(ones, slab, PLAIN)[:ROWS]
    for k in range(NX):
        cross_out[k, :TILE] = raw[:, k * SLAB : (k + 1) * SLAB]
        cross_out[k, TILE:] = total[:, k * SLAB : (k + 1) * SLAB]
    cross_in[x] = cross_out[x]

    def cross_to(d):
        at = x_at(d)
        return copy(cross_out.at[at], cross_in.at[x], cross_s.at[d], cross_r.at[x], in_x(at))

    def cross_from(d):
        at = x_at(d)
        return copy(cross_out.at[at], cross_in.at[at], cross_s.at[d], cross_r.at[at], in_x(at))

    each(NX, lambda d: cross_to(d).start())

    each(NX, lambda d: gram_from(d).wait_recv())
    gram = grams[0]
    for k in range(1, NX):
        gram = gram + grams[k]
    mean_pred = jnp.broadcast_to(gram[TILE // 2 : TILE // 2 + 1] / ensemble, (TILE, TILE))
    mean_turned = mean_pred.T
    gram = unfolded(gram[: TILE // 2], gram[TILE // 2 + ROWS :])
    system = (gram - ensemble * mean_turned * mean_pred) * coupled[...] + spread[...]

    inverted = inverse_blocks(system, 0, TILE // PANEL // 4)

    each(NX, lambda d: cross_from(d).wait_recv())
    cross = cross_in[0]
    for k in range(1, NX):
        cross = cross + cross_in[k]
    mean_param = cross[TILE : TILE + 1] / ensemble
    crosses[x] = cross[:TILE] - ensemble * mean_turned * mean_param

    def crosses_to(d):
        return copy(crosses.at[x], crosses.at[x], crosses_s.at[d], crosses_r.at[x], in_x(x_at(d)))

    def crosses_from(d):
        at = x_at(d)
        return copy(crosses.at[at], crosses.at[at], crosses_s.at[d], crosses_r.at[at], in_x(at))

    each(NX, lambda d: crosses_to(d).start())

    each(nz, lambda d: pert_from(d).wait_recv())
    noise_root = jnp.sqrt(noise[...])
    for t, d in enumerate(turns_z):
        at = z_at(d)
        left = observed[...] + noise_root * perts[at].astype(F32) - preds[at].astype(F32)
        for k in range(no):
            innov[k % 2, k // 2, t * ROWS : (t + 1) * ROWS, :] = left[k * ROWS : (k + 1) * ROWS]

    inverted = inverse_blocks(inverted, TILE // PANEL // 4, TILE // PANEL)

    each(NX, lambda d: crosses_from(d).wait_recv())
    cross = jnp.concatenate([crosses[k] for k in range(NX)], axis=1)
    gain = dot(inverted, cross, PLAIN, lax.Precision.HIGHEST) / (ensemble - 1)
    high = gain.astype(BF16)
    low = (gain - high.astype(F32)).astype(BF16)
    weights = jnp.concatenate([high, low], axis=1)
    weights = jnp.concatenate([weights, weights], axis=0)

    def share(core, d):
        left = innov[core, y_at(d)]
        big = left.astype(BF16)
        small = (left - big.astype(F32)).astype(BF16)
        parts = dot(jnp.concatenate([big, small], axis=1), weights, PLAIN)
        return parts[:, :width] + parts[:, width:]

    def pair_copy(d):
        return copy(pair_out.at[d], pair_in.at[d], pair_s.at[d], pair_r.at[d], (g, sibling))

    def share_to(d, h):
        span = pl.ds(h * fore, fore)
        to = (g, y_at(d) * 2 + c)
        return copy(share_out.at[d, span], share_in.at[y, span], share_s.at[d, h], share_r.at[y, h], to)

    def share_from(d, h):
        at = y_at(d)
        span = pl.ds(h * fore, fore)
        return copy(share_out.at[d, span], share_in.at[at, span], share_s.at[d, h], share_r.at[at, h], (g, at * 2 + c))

    def incr_to(t):
        at = z_at(turns_z[t])
        return copy(incr_out.at[t], final.at[z], incr_s.at[t], incr_r.at[z], in_z(at))

    def incr_from(d):
        at = z_at(d)
        return copy(incr_out.at[0], final.at[at], incr_s.at[0], incr_r.at[at], in_z(at))

    for d in turns:
        pair_out[d] = share(1 - c, d).astype(BF16)
        pair_copy(d).start()
    mine = {d: share(c, d) for d in turns}
    for d in turns:
        pair_copy(d).wait_recv()
        total = mine[d] + pair_in[d].astype(F32)
        if d:
            share_out[d] = total.astype(BF16)
            share_to(d, 0).start()
    for d in turns[:-1]:
        share_to(d, 1).start()
    for h in range(2):
        part = total[h * fore : (h + 1) * fore]
        for d in turns[:-1]:
            share_from(d, h).wait_recv()
            part = part + share_in[y_at(d), h * fore : (h + 1) * fore].astype(F32)
        for t in range(h * nz // 2, (h + 1) * nz // 2):
            first = t * ROWS - h * fore
            incr_out[t] = part[first : first + ROWS]
            if t < nz - 1:
                incr_to(t).start()
    final[z] = incr_out[nz - 1]
    each(nz, lambda d: incr_from(d).wait_recv())
    for k in range(nz):
        at = slice(k * width, (k + 1) * width)
        out[:, at] = members[:, at].astype(F32) + final[k]

    def y_sent(d):
        slab_to(d).wait_send()
        slab_pass(d).wait_send()
        share_to(d, 0).wait_send()
        share_to(d, 1).wait_send()
        pair_copy(d).wait_send()

    def z_sent(d):
        block_to(d).wait_send()
        pert_to(d).wait_send()
        pred_to(d).wait_send()

    def x_sent(d):
        gram_to(d).wait_send()
        cross_to(d).wait_send()
        crosses_to(d).wait_send()

    each(no, lambda d: rows_to(d).wait_send())
    half_copy.wait_send()
    slab_own.wait_send()
    pair_copy(0).wait_send()
    each(ny, y_sent)
    each(nz, z_sent)
    for t in range(nz - 1):
        incr_to(t).wait_send()
    each(NX, x_sent)


def shards(members, alphas, points, labels, noise, observed, perturb):
    nm, no = lax.axis_size("mem"), lax.axis_size("obs")
    nz, ny = nm // NX, no // 2
    coeffs = members.shape[1]
    dims = alphas.shape[0]
    side, width = nz * ROWS, coeffs // nz
    vmem, many = pltpu.VMEM, pltpu.SemaphoreType.DMA
    signal = pltpu.SemaphoreType.REGULAR
    return pl.pallas_call(
        lambda *refs: kernel(nm, no, *refs),
        out_shape=jax.ShapeDtypeStruct((ROWS, coeffs), F32),
        in_specs=[pl.BlockSpec(memory_space=pl.ANY)] * 7,
        out_specs=pl.BlockSpec(memory_space=vmem),
        scratch_shapes=[
            vmem((ROWS, coeffs), BF16),
            vmem((dims, coeffs), jnp.int32),
            vmem((dims, 2 * TILE), F32),
            vmem((1, TILE), jnp.int32),
            vmem((1, TILE), F32),
            vmem((1, TILE), F32),
            vmem((2, 2 * ROWS, coeffs // 4), BF16),
            vmem((no, 2 * ROWS, coeffs // 4), BF16),
            vmem((2, no * ROWS, TILE), F32),
            vmem((no * ROWS, TILE), F32),
            vmem((nz, 2 * ROWS, width // 2), BF16),
            vmem((nz, 2 * ROWS, width // 2), BF16),
            vmem((no, side, width), BF16),
            vmem((nz, no * ROWS, TILE), BF16),
            vmem((nz, no * ROWS, TILE), BF16),
            vmem((NX, TILE // 2 + 2 * ROWS, TILE), F32),
            vmem((2, dims, 3, TILE, TILE), F32),
            vmem((4 * TILE, coeffs // 4), BF16),
            vmem((2, ny, side, TILE), F32),
            vmem((no, side, TILE), F32),
            vmem((NX, TILE + ROWS, SLAB), F32),
            vmem((NX, TILE + ROWS, SLAB), F32),
            vmem((NX, TILE, SLAB), F32),
            vmem((ny, side, width), BF16),
            vmem((ny, side, width), BF16),
            vmem((ny, side, width), BF16),
            vmem((ny, side, width), BF16),
            vmem((nz, ROWS, width), F32),
            vmem((nz, ROWS, width), F32),
            vmem((TILE, TILE), F32),
            vmem((TILE, TILE), F32),
            signal,
            many((7,)),
            many((no,)),
            many((no,)),
            many,
            many,
            many((nz,)),
            many((nz,)),
            many((no,)),
            many((no,)),
            many((nz,)),
            many((nz,)),
            many((nz,)),
            many((nz,)),
            many((NX,)),
            many((NX,)),
            many((NX,)),
            many((NX,)),
            many((NX,)),
            many((NX,)),
            many((ny,)),
            many((ny,)),
            many((ny, 2)),
            many((ny, 2)),
            many((nz,)),
            many((nz,)),
        ],
        compiler_params=pltpu.CompilerParams(
            collective_id=0, has_side_effects=True, vmem_limit_bytes=60 * 1024 * 1024
        ),
    )(members, alphas, points, labels.reshape(1, TILE), noise.reshape(1, TILE), observed.reshape(1, TILE), perturb)


def solution(mesh):
    in_specs = (P(("mem", "obs"), None), P(), P(), P("obs"), P("obs"), P("obs"), P("mem", "obs"))
    out_specs = P(("mem", "obs"), None)
    return jax.shard_map(shards, mesh=mesh, in_specs=in_specs, out_specs=out_specs, check_vma=False)
```

```python
import math

import jax
import jax.numpy as jnp
from jax import lax
from jax.experimental import pallas as pl
from jax.experimental.pallas import tpu as pltpu
from jax.sharding import PartitionSpec as P

ROWS = 8
TILE = 128
SLAB = 128
PANEL = 8
CHUNK = 256
NX = 4
F32 = jnp.float32
BF16 = jnp.bfloat16
FIRST = (((0,), (0,)), ((), ()))
LAST = (((1,), (1,)), ((), ()))
PLAIN = (((1,), (0,)), ((), ()))


def dot(left, right, dims, precision=None):
    return lax.dot_general(left, right, dims, precision=precision, preferred_element_type=F32)


def inverse_blocks(matrix, first, last):
    size = matrix.shape[0]
    row = lax.broadcasted_iota(jnp.int32, (PANEL, size), 0)
    lane = lax.broadcasted_iota(jnp.int32, (PANEL, size), 1)
    rest_lane = lax.broadcasted_iota(jnp.int32, (size - PANEL, size), 1)
    unit = jnp.where(lane == row, 1.0, 0.0).astype(F32)

    def block(_, full):
        top, rest = full[:PANEL], full[PANEL:]
        column = [jnp.broadcast_to(top[:, j : j + 1], (PANEL, size)) for j in range(PANEL)]
        panel = jnp.where(lane < PANEL, unit, top)
        for p in range(PANEL):
            scale = 1.0 / column[p][p : p + 1]
            pivot = panel[p : p + 1] * scale
            panel = jnp.where(row == p, pivot, panel - column[p] * pivot)
            for j in range(p + 1, PANEL):
                entry = column[j][p : p + 1] * scale
                column[j] = jnp.where(row == p, entry, column[j] - column[p] * entry)
        update = jnp.where(rest_lane < PANEL, 0.0, rest)
        for j in range(PANEL):
            update = update - rest[:, j : j + 1] * panel[j : j + 1]
        return pltpu.roll(jnp.concatenate([update, panel], axis=0), size - PANEL, 1)

    return lax.fori_loop(first, last, block, matrix)


def places(rows):
    shape = (rows, TILE)
    return lax.broadcasted_iota(jnp.int32, shape, 0), lax.broadcasted_iota(jnp.int32, shape, 1)


def folded(square):
    edge = TILE // 2
    row, lane = places(edge)
    return jnp.where(lane >= row, square[:edge], pltpu.roll(square[edge:], edge, 1))


def diagonal_row(square):
    row, lane = places(TILE)
    kept = jnp.sum(jnp.where(row == lane, square, 0.0), axis=0, keepdims=True)
    return jnp.broadcast_to(kept, (ROWS, TILE))


def unfolded(half, kept):
    edge = TILE // 2
    row, lane = places(TILE)
    whole = jnp.concatenate([half, pltpu.roll(half, edge, 1)], axis=0)
    direct = jnp.where(row < edge, lane - row, jnp.where(lane >= edge, row - lane - 1, -1)) >= 0
    square = jnp.where(direct, whole, whole.T)
    return jnp.where((row == lane) & (row >= edge), jnp.broadcast_to(kept[:1], (TILE, TILE)), square)


def kernel(
    nm,
    no,
    members_hbm,
    alphas_hbm,
    points_hbm,
    labels_hbm,
    noise_hbm,
    observed_hbm,
    perturb_hbm,
    out,
    members,
    alphas,
    points,
    labels,
    noise,
    observed,
    rows_out,
    rows_in,
    halves,
    half_in,
    blocks_out,
    blocks_in,
    slabs,
    preds,
    perts,
    grams,
    table,
    basis,
    innov,
    prior,
    cross_out,
    cross_in,
    crosses,
    pair_out,
    pair_in,
    share_out,
    share_in,
    incr_out,
    final,
    coupled,
    spread,
    ready,
    local_s,
    rows_s,
    rows_r,
    half_s,
    half_r,
    blocks_s,
    blocks_r,
    slabs_s,
    slabs_r,
    preds_s,
    preds_r,
    perts_s,
    perts_r,
    grams_s,
    grams_r,
    cross_s,
    cross_r,
    crosses_s,
    crosses_r,
    pair_s,
    pair_r,
    share_s,
    share_r,
    incr_s,
    incr_r,
):
    g, o = lax.axis_index("mem"), lax.axis_index("obs")
    z, x = lax.div(g, NX), lax.rem(g, NX)
    y, c = lax.div(o, 2), lax.rem(o, 2)
    nz, ny = nm // NX, no // 2
    coeffs = members.shape[1]
    half = coeffs // 2
    quarter = half // 2
    width = coeffs // nz
    chunk = min(CHUNK, quarter)
    ensemble = nm * no * ROWS
    line = nz * no * ROWS
    side = nz * ROWS
    mesh = pl.DeviceIdType.MESH

    def obs_at(d):
        return lax.rem(o + d, no)

    def z_at(d):
        return lax.rem(z + d, nz)

    def x_at(d):
        return lax.rem(x + d, NX)

    def y_at(d):
        return lax.rem(y + d, ny)

    def in_z(at):
        return (at * NX + x, o)

    def in_x(at):
        return (z * NX + at, o)

    sibling = y * 2 + 1 - c

    def copy(src, dst, send, recv, to):
        return pltpu.make_async_remote_copy(
            src_ref=src, dst_ref=dst, send_sem=send, recv_sem=recv, device_id=to, device_id_type=mesh
        )

    def tell(semaphore, to):
        pl.semaphore_signal(semaphore, inc=1, device_id=to, device_id_type=mesh)

    def each(count, act):
        def step(d, carry):
            act(d)
            return carry

        lax.fori_loop(1, count, step, 0)

    far = sorted(range(1, nz), key=lambda d: -min(d, nz - d))

    turns_z = far + [0]
    turns = sorted(range(1, ny), key=lambda d: -min(d, ny - d)) + [0]
    fore = side // 2

    fetch = [
        pltpu.make_async_copy(src, dst, local_s.at[k])
        for k, (src, dst) in enumerate(
            (
                (members_hbm, members),
                (points_hbm.at[:, pl.ds(pl.multiple_of(y * 2 * TILE, 2 * TILE), 2 * TILE)], points),
                (labels_hbm, labels),
                (noise_hbm, noise),
                (observed_hbm, observed),
                (perturb_hbm, perts.at[z]),
                (alphas_hbm, alphas),
            )
        )
    ]
    for f in fetch:
        f.start()

    barrier = pltpu.get_barrier_semaphore()
    reach = range(1, nz // 4 + 1)
    near = [in_z(z_at(s * k % nz)) for k in reach for s in (1, -1)]
    each(no, lambda d: tell(barrier, (g, obs_at(d))))
    each(NX, lambda d: tell(barrier, in_x(x_at(d))))
    for to in near:
        tell(barrier, to)

    fetch[0].wait()
    own = members[...].astype(F32)
    for h in range(2):
        part = own[:, h * half : (h + 1) * half]
        rows_out[h] = jnp.concatenate([part[:, :quarter], part[:, quarter:]], axis=0).astype(BF16)
    rows_in[o] = rows_out[c]
    for k in range(nz):
        part = own[:, k * width : (k + 1) * width]
        blocks_out[k] = jnp.concatenate([part[:, : width // 2], part[:, width // 2 :]], axis=0).astype(BF16)
    blocks_in[z] = blocks_out[z]

    pl.semaphore_wait(barrier, no - 1 + NX - 1 + len(near))

    def rows_to(d):
        to = obs_at(d)
        return copy(rows_out.at[lax.rem(to, 2)], rows_in.at[o], rows_s.at[d], rows_r.at[o], (g, to))

    def rows_from(d):
        at = obs_at(d)
        return copy(rows_out.at[c], rows_in.at[at], rows_s.at[d], rows_r.at[at], (g, at))

    for d in sorted(range(1, no), key=lambda d: -min(d, no - d)):
        rows_to(d).start()
    for to in near[-2:]:
        tell(ready, to)

    fetch[1].wait()

    def tabulate(t):
        at = points[:, t * TILE : (t + 1) * TILE]
        turned = jnp.concatenate([at, jnp.zeros((TILE - at.shape[0], TILE), F32)], axis=0).T
        for d in range(at.shape[0]):
            value = jnp.broadcast_to(turned[:, d : d + 1], (TILE, TILE))
            second = value * value - 1.0
            third = value * second - 2.0 * value
            table[t, d, 0] = value
            table[t, d, 1] = second * (1.0 / math.sqrt(2.0))
            table[t, d, 2] = third * (1.0 / math.sqrt(6.0))

    tabulate(0)
    tabulate(1)

    for f in fetch[2:]:
        f.wait()
    label = jnp.broadcast_to(labels[...].astype(F32), (TILE, TILE))
    diagonal = lax.broadcasted_iota(jnp.int32, (TILE, TILE), 0) == lax.broadcasted_iota(jnp.int32, (TILE, TILE), 1)
    coupled[...] = jnp.where(label == label.T, 1.0 / (ensemble - 1), 0.0).astype(F32)
    spread[...] = jnp.where(diagonal, jnp.broadcast_to(noise[...], (TILE, TILE)), 0.0)

    def basis_part(first_step, last_step):
        def step(n, carry):
            per = quarter // chunk
            q, t, k = lax.div(n, 2 * per), lax.rem(lax.div(n, per), 2), lax.rem(n, per)
            first = pl.multiple_of(k * chunk, chunk)
            degree = alphas[:, pl.ds(pl.multiple_of(c * half + q * quarter + first, chunk), chunk)]
            product = None
            for d in range(degree.shape[0]):
                odd = (degree[d : d + 1] & 1) == 1
                high = degree[d : d + 1] >= 2
                one, two, three = (jnp.concatenate([table[t, d, p]] * (chunk // TILE), axis=1) for p in range(3))
                value = jnp.where(high, jnp.where(odd, three, two), jnp.where(odd, one, 1.0))
                product = value if product is None else product * value
            place = pl.multiple_of((q * 2 + t) * TILE, TILE)
            basis[pl.ds(place, TILE), pl.ds(first, chunk)] = product.astype(BF16)
            return carry

        lax.fori_loop(first_step, last_step, step, 0)

    steps = 4 * (quarter // chunk)
    basis_part(0, steps // 8)
    pl.semaphore_wait(ready, 2)

    def block_to(d):
        return copy(blocks_out.at[z_at(d)], blocks_in.at[z], blocks_s.at[d], blocks_r.at[z], in_z(z_at(d)))

    def block_from(d):
        at = z_at(d)
        return copy(blocks_out.at[at], blocks_in.at[at], blocks_s.at[d], blocks_r.at[at], in_z(at))

    def pert_to(d):
        return copy(perts.at[z], perts.at[z], perts_s.at[d], perts_r.at[z], in_z(z_at(d)))

    def pert_from(d):
        at = z_at(d)
        return copy(perts.at[at], perts.at[at], perts_s.at[d], perts_r.at[at], in_z(at))

    for d in far:
        block_to(d).start()
    basis_part(steps // 8, steps)

    each(no, lambda d: rows_from(d).wait_recv())
    both = dot(rows_in[...].reshape(no * 2 * ROWS, quarter), basis[...], LAST)
    both = both.reshape(no, 2, ROWS, 4 * TILE)
    part = (both[:, 0, :, : 2 * TILE] + both[:, 1, :, 2 * TILE :]).reshape(no * ROWS, 2 * TILE)
    for t in range(2):
        halves[t] = part[:, t * TILE : (t + 1) * TILE]
    half_copy = copy(halves.at[1 - c], half_in, half_s, half_r, (g, sibling))
    half_copy.start()
    half_copy.wait_recv()
    preds[z] = (halves[c] + half_in[...]).astype(BF16)

    def pred_to(d):
        return copy(preds.at[z], preds.at[z], preds_s.at[d], preds_r.at[z], in_z(z_at(d)))

    def pred_from(d):
        at = z_at(d)
        return copy(preds.at[at], preds.at[at], preds_s.at[d], preds_r.at[at], in_z(at))

    for d in far:
        pred_to(d).start()

    each(nz, lambda d: block_from(d).wait_recv())
    block = blocks_in[...].astype(F32)
    block = jnp.concatenate([block[:, :ROWS], block[:, ROWS:]], axis=2)
    slabs[o] = block.reshape(side, width).astype(BF16)

    def slab_to(d):
        return copy(slabs.at[o], slabs.at[o], slabs_s.at[d], slabs_r.at[o], (g, y_at(d) * 2 + c))

    def slab_from(at, to):
        return copy(slabs.at[at], slabs.at[at], slabs_s.at[0], slabs_r.at[at], (g, to))

    def slab_pass(d):
        at = y_at(d) * 2 + c
        return copy(slabs.at[at], slabs.at[at], slabs_s.at[ny + d], slabs_r.at[at], (g, sibling))

    slab_own = copy(slabs.at[o], slabs.at[o], slabs_s.at[0], slabs_r.at[o], (g, sibling))
    each(ny, lambda d: slab_to(d).start())
    slab_own.start()

    def pass_on(d):
        at = y_at(d) * 2 + c
        slab_from(at, at).wait_recv()
        slab_pass(d).start()

    each(ny, pass_on)

    each(nz, lambda d: pred_from(d).wait_recv())
    flat = preds[...].reshape(line, TILE)
    ones = jnp.ones((2 * ROWS, line), BF16)
    gram = dot(flat, flat, FIRST)
    grams[x] = jnp.concatenate([folded(gram), dot(ones, flat, PLAIN)[:ROWS], diagonal_row(gram)], axis=0)

    def gram_to(d):
        return copy(grams.at[x], grams.at[x], grams_s.at[d], grams_r.at[x], in_x(x_at(d)))

    def gram_from(d):
        at = x_at(d)
        return copy(grams.at[at], grams.at[at], grams_s.at[d], grams_r.at[at], in_x(at))

    for d in sorted(range(1, NX), key=lambda d: -min(d, NX - d)):
        gram_to(d).start()
    for d in far:
        pert_to(d).start()

    for t in range(nz):
        value = preds[t].astype(F32)
        for k in range(no):
            prior[k, t * ROWS : (t + 1) * ROWS, :] = value[k * ROWS : (k + 1) * ROWS]
    ordered = prior[...].reshape(line, TILE).astype(BF16)

    slab_from(sibling, sibling).wait_recv()
    each(ny, lambda d: slab_from(y_at(d) * 2 + 1 - c, sibling).wait_recv())
    slab = slabs[...].reshape(line, width)
    raw = dot(ordered, slab, FIRST)
    total = dot(ones, slab, PLAIN)[:ROWS]
    for k in range(NX):
        cross_out[k, :ROWS] = total[:, k * SLAB : (k + 1) * SLAB]
        cross_out[k, ROWS:] = raw[:, k * SLAB : (k + 1) * SLAB]
    cross_in[x] = cross_out[x]

    def piece(h):
        return pl.ds(h * (TILE // 2 + ROWS), TILE // 2 + ROWS * (1 - h))

    def cross_to(d, h):
        at = x_at(d)
        return copy(cross_out.at[at, piece(h)], cross_in.at[x, piece(h)], cross_s.at[d, h], cross_r.at[x, h], in_x(at))

    def cross_from(d, h):
        at = x_at(d)
        return copy(cross_out.at[at, piece(h)], cross_in.at[at, piece(h)], cross_s.at[d, h], cross_r.at[at, h], in_x(at))

    for h in range(2):
        for d in sorted(range(1, NX), key=lambda d: -min(d, NX - d)):
            cross_to(d, h).start()

    each(NX, lambda d: gram_from(d).wait_recv())
    gram = grams[0]
    for k in range(1, NX):
        gram = gram + grams[k]
    mean_pred = jnp.broadcast_to(gram[TILE // 2 : TILE // 2 + 1] / ensemble, (TILE, TILE))
    mean_turned = mean_pred.T
    gram = unfolded(gram[: TILE // 2], gram[TILE // 2 + ROWS :])
    system = (gram - ensemble * mean_turned * mean_pred) * coupled[...] + spread[...]

    inverted = inverse_blocks(system, 0, TILE // PANEL // 4)

    def crosses_to(d, h):
        span = crosses.at[x, pl.ds(h * TILE // 2, TILE // 2)]
        return copy(span, span, crosses_s.at[d, h], crosses_r.at[x, h], in_x(x_at(d)))

    def crosses_from(d, h):
        at = x_at(d)
        span = crosses.at[at, pl.ds(h * TILE // 2, TILE // 2)]
        return copy(span, span, crosses_s.at[d, h], crosses_r.at[at, h], in_x(at))

    mean_param = None
    for h in range(2):
        for d in range(1, NX):
            cross_from(d, h).wait_recv()
        cross = cross_in[0, piece(h)]
        for k in range(1, NX):
            cross = cross + cross_in[k, piece(h)]
        if h == 0:
            mean_param = cross[:1] / ensemble
            cross = cross[ROWS:]
        part = slice(h * TILE // 2, (h + 1) * TILE // 2)
        crosses[x, part] = cross - ensemble * mean_turned[part] * mean_param
        for d in sorted(range(1, NX), key=lambda d: -min(d, NX - d)):
            crosses_to(d, h).start()
        if h == 0:
            inverted = inverse_blocks(inverted, TILE // PANEL // 4, TILE // PANEL // 2)

    each(nz, lambda d: pert_from(d).wait_recv())
    noise_root = jnp.sqrt(noise[...])
    for t, d in enumerate(turns_z):
        at = z_at(d)
        left = observed[...] + noise_root * perts[at].astype(F32) - preds[at].astype(F32)
        for k in range(no):
            innov[k % 2, k // 2, t * ROWS : (t + 1) * ROWS, :] = left[k * ROWS : (k + 1) * ROWS]

    inverted = inverse_blocks(inverted, TILE // PANEL // 2, TILE // PANEL)

    for h in range(2):
        for d in range(1, NX):
            crosses_from(d, h).wait_recv()
    cross = jnp.concatenate([crosses[k] for k in range(NX)], axis=1)
    gain = dot(inverted, cross, PLAIN, lax.Precision.HIGHEST) / (ensemble - 1)
    high = gain.astype(BF16)
    low = (gain - high.astype(F32)).astype(BF16)
    weights = jnp.concatenate([high, low], axis=1)
    weights = jnp.concatenate([weights, weights], axis=0)

    def share(core, d):
        left = innov[core, y_at(d)]
        big = left.astype(BF16)
        small = (left - big.astype(F32)).astype(BF16)
        parts = dot(jnp.concatenate([big, small], axis=1), weights, PLAIN)
        return parts[:, :width] + parts[:, width:]

    def pair_copy(d):
        return copy(pair_out.at[d], pair_in.at[d], pair_s.at[d], pair_r.at[d], (g, sibling))

    def share_to(d, h):
        span = pl.ds(h * fore, fore)
        to = (g, y_at(d) * 2 + c)
        return copy(share_out.at[d, span], share_in.at[y, span], share_s.at[d, h], share_r.at[y, h], to)

    def share_from(d, h):
        at = y_at(d)
        span = pl.ds(h * fore, fore)
        return copy(share_out.at[d, span], share_in.at[at, span], share_s.at[d, h], share_r.at[at, h], (g, at * 2 + c))

    def incr_to(t):
        at = z_at(turns_z[t])
        return copy(incr_out.at[t], final.at[z], incr_s.at[t], incr_r.at[z], in_z(at))

    def incr_from(d):
        at = z_at(d)
        return copy(incr_out.at[0], final.at[at], incr_s.at[0], incr_r.at[at], in_z(at))

    for d in turns:
        pair_out[d] = share(1 - c, d).astype(BF16)
        pair_copy(d).start()
    mine = {d: share(c, d) for d in turns}
    for d in turns:
        pair_copy(d).wait_recv()
        total = mine[d] + pair_in[d].astype(F32)
        if d:
            share_out[d] = total.astype(BF16)
            share_to(d, 0).start()
    for d in turns[:-1]:
        share_to(d, 1).start()
    for h in range(2):
        part = total[h * fore : (h + 1) * fore]
        for d in turns[:-1]:
            share_from(d, h).wait_recv()
            part = part + share_in[y_at(d), h * fore : (h + 1) * fore].astype(F32)
        for t in range(h * nz // 2, (h + 1) * nz // 2):
            first = t * ROWS - h * fore
            incr_out[t] = part[first : first + ROWS]
            if t < nz - 1:
                incr_to(t).start()
    final[z] = incr_out[nz - 1]
    def y_sent(d):
        slab_to(d).wait_send()
        slab_pass(d).wait_send()
        share_to(d, 0).wait_send()
        share_to(d, 1).wait_send()
        pair_copy(d).wait_send()

    def z_sent(d):
        block_to(d).wait_send()
        pert_to(d).wait_send()
        pred_to(d).wait_send()

    def x_sent(d):
        gram_to(d).wait_send()
        for h in range(2):
            cross_to(d, h).wait_send()
            crosses_to(d, h).wait_send()

    each(no, lambda d: rows_to(d).wait_send())
    half_copy.wait_send()
    slab_own.wait_send()
    pair_copy(0).wait_send()
    each(ny, y_sent)
    each(nz, z_sent)
    for d in reversed(turns_z):
        at = z_at(d)
        if d:
            incr_from(d).wait_recv()
        place = pl.ds(pl.multiple_of(at * width, width), width)
        out[:, place] = members[:, place].astype(F32) + final[at]

    for t in range(nz - 1):
        incr_to(t).wait_send()
    each(NX, x_sent)


def shards(members, alphas, points, labels, noise, observed, perturb):
    nm, no = lax.axis_size("mem"), lax.axis_size("obs")
    nz, ny = nm // NX, no // 2
    coeffs = members.shape[1]
    dims = alphas.shape[0]
    side, width = nz * ROWS, coeffs // nz
    vmem, many = pltpu.VMEM, pltpu.SemaphoreType.DMA
    signal = pltpu.SemaphoreType.REGULAR
    return pl.pallas_call(
        lambda *refs: kernel(nm, no, *refs),
        out_shape=jax.ShapeDtypeStruct((ROWS, coeffs), F32),
        in_specs=[pl.BlockSpec(memory_space=pl.ANY)] * 7,
        out_specs=pl.BlockSpec(memory_space=vmem),
        scratch_shapes=[
            vmem((ROWS, coeffs), BF16),
            vmem((dims, coeffs), jnp.int32),
            vmem((dims, 2 * TILE), F32),
            vmem((1, TILE), jnp.int32),
            vmem((1, TILE), F32),
            vmem((1, TILE), F32),
            vmem((2, 2 * ROWS, coeffs // 4), BF16),
            vmem((no, 2 * ROWS, coeffs // 4), BF16),
            vmem((2, no * ROWS, TILE), F32),
            vmem((no * ROWS, TILE), F32),
            vmem((nz, 2 * ROWS, width // 2), BF16),
            vmem((nz, 2 * ROWS, width // 2), BF16),
            vmem((no, side, width), BF16),
            vmem((nz, no * ROWS, TILE), BF16),
            vmem((nz, no * ROWS, TILE), BF16),
            vmem((NX, TILE // 2 + 2 * ROWS, TILE), F32),
            vmem((2, dims, 3, TILE, TILE), F32),
            vmem((4 * TILE, coeffs // 4), BF16),
            vmem((2, ny, side, TILE), F32),
            vmem((no, side, TILE), F32),
            vmem((NX, TILE + ROWS, SLAB), F32),
            vmem((NX, TILE + ROWS, SLAB), F32),
            vmem((NX, TILE, SLAB), F32),
            vmem((ny, side, width), BF16),
            vmem((ny, side, width), BF16),
            vmem((ny, side, width), BF16),
            vmem((ny, side, width), BF16),
            vmem((nz, ROWS, width), F32),
            vmem((nz, ROWS, width), F32),
            vmem((TILE, TILE), F32),
            vmem((TILE, TILE), F32),
            signal,
            many((7,)),
            many((no,)),
            many((no,)),
            many,
            many,
            many((nz,)),
            many((nz,)),
            many((no,)),
            many((no,)),
            many((nz,)),
            many((nz,)),
            many((nz,)),
            many((nz,)),
            many((NX,)),
            many((NX,)),
            many((NX, 2)),
            many((NX, 2)),
            many((NX, 2)),
            many((NX, 2)),
            many((ny,)),
            many((ny,)),
            many((ny, 2)),
            many((ny, 2)),
            many((nz,)),
            many((nz,)),
        ],
        compiler_params=pltpu.CompilerParams(
            collective_id=0, has_side_effects=True, vmem_limit_bytes=60 * 1024 * 1024
        ),
    )(members, alphas, points, labels.reshape(1, TILE), noise.reshape(1, TILE), observed.reshape(1, TILE), perturb)


def solution(mesh):
    in_specs = (P(("mem", "obs"), None), P(), P(), P("obs"), P("obs"), P("obs"), P("mem", "obs"))
    out_specs = P(("mem", "obs"), None)
    return jax.shard_map(shards, mesh=mesh, in_specs=in_specs, out_specs=out_specs, check_vma=False)
```

```python
import math

import jax
import jax.numpy as jnp
from jax import lax
from jax.experimental import pallas as pl
from jax.experimental.pallas import tpu as pltpu
from jax.sharding import PartitionSpec as P

ROWS = 8
TILE = 128
SLAB = 128
PANEL = 8
CHUNK = 256
NX = 4
F32 = jnp.float32
BF16 = jnp.bfloat16
FIRST = (((0,), (0,)), ((), ()))
LAST = (((1,), (1,)), ((), ()))
PLAIN = (((1,), (0,)), ((), ()))


def dot(left, right, dims, precision=None):
    return lax.dot_general(left, right, dims, precision=precision, preferred_element_type=F32)


def inverse_blocks(matrix, first, last):
    size = matrix.shape[0]
    row = lax.broadcasted_iota(jnp.int32, (PANEL, size), 0)
    lane = lax.broadcasted_iota(jnp.int32, (PANEL, size), 1)
    rest_lane = lax.broadcasted_iota(jnp.int32, (size - PANEL, size), 1)
    unit = jnp.where(lane == row, 1.0, 0.0).astype(F32)

    def block(_, full):
        top, rest = full[:PANEL], full[PANEL:]
        column = [jnp.broadcast_to(top[:, j : j + 1], (PANEL, size)) for j in range(PANEL)]
        panel = jnp.where(lane < PANEL, unit, top)
        for p in range(PANEL):
            scale = 1.0 / column[p][p : p + 1]
            pivot = panel[p : p + 1] * scale
            panel = jnp.where(row == p, pivot, panel - column[p] * pivot)
            for j in range(p + 1, PANEL):
                entry = column[j][p : p + 1] * scale
                column[j] = jnp.where(row == p, entry, column[j] - column[p] * entry)
        update = jnp.where(rest_lane < PANEL, 0.0, rest)
        for j in range(PANEL):
            update = update - rest[:, j : j + 1] * panel[j : j + 1]
        return pltpu.roll(jnp.concatenate([update, panel], axis=0), size - PANEL, 1)

    return lax.fori_loop(first, last, block, matrix)


def places(rows):
    shape = (rows, TILE)
    return lax.broadcasted_iota(jnp.int32, shape, 0), lax.broadcasted_iota(jnp.int32, shape, 1)


def folded(square):
    edge = TILE // 2
    row, lane = places(edge)
    return jnp.where(lane >= row, square[:edge], pltpu.roll(square[edge:], edge, 1))


def diagonal_row(square):
    row, lane = places(TILE)
    kept = jnp.sum(jnp.where(row == lane, square, 0.0), axis=0, keepdims=True)
    return jnp.broadcast_to(kept, (ROWS, TILE))


def unfolded(half, kept):
    edge = TILE // 2
    row, lane = places(TILE)
    whole = jnp.concatenate([half, pltpu.roll(half, edge, 1)], axis=0)
    direct = jnp.where(row < edge, lane - row, jnp.where(lane >= edge, row - lane - 1, -1)) >= 0
    square = jnp.where(direct, whole, whole.T)
    return jnp.where((row == lane) & (row >= edge), jnp.broadcast_to(kept[:1], (TILE, TILE)), square)


def kernel(
    nm,
    no,
    members_hbm,
    alphas_hbm,
    points_hbm,
    labels_hbm,
    noise_hbm,
    observed_hbm,
    perturb_hbm,
    out,
    members,
    alphas,
    points,
    labels,
    noise,
    observed,
    rows_out,
    rows_in,
    halves,
    half_in,
    blocks_out,
    blocks_in,
    slabs,
    preds,
    perts,
    grams,
    table,
    basis,
    innov,
    prior,
    cross_out,
    cross_in,
    crosses,
    pair_out,
    pair_in,
    share_out,
    share_in,
    incr_out,
    final,
    coupled,
    spread,
    ready,
    local_s,
    rows_s,
    rows_r,
    half_s,
    half_r,
    blocks_s,
    blocks_r,
    slabs_s,
    slabs_r,
    preds_s,
    preds_r,
    perts_s,
    perts_r,
    grams_s,
    grams_r,
    cross_s,
    cross_r,
    crosses_s,
    crosses_r,
    pair_s,
    pair_r,
    share_s,
    share_r,
    incr_s,
    incr_r,
):
    g, o = lax.axis_index("mem"), lax.axis_index("obs")
    z, x = lax.div(g, NX), lax.rem(g, NX)
    y, c = lax.div(o, 2), lax.rem(o, 2)
    nz, ny = nm // NX, no // 2
    coeffs = members.shape[1]
    half = coeffs // 2
    quarter = half // 2
    width = coeffs // nz
    chunk = min(CHUNK, quarter)
    ensemble = nm * no * ROWS
    line = nz * no * ROWS
    side = nz * ROWS
    mesh = pl.DeviceIdType.MESH

    def obs_at(d):
        return lax.rem(o + d, no)

    def z_at(d):
        return lax.rem(z + d, nz)

    def x_at(d):
        return lax.rem(x + d, NX)

    def y_at(d):
        return lax.rem(y + d, ny)

    def in_z(at):
        return (at * NX + x, o)

    def in_x(at):
        return (z * NX + at, o)

    sibling = y * 2 + 1 - c

    def copy(src, dst, send, recv, to):
        return pltpu.make_async_remote_copy(
            src_ref=src, dst_ref=dst, send_sem=send, recv_sem=recv, device_id=to, device_id_type=mesh
        )

    def tell(semaphore, to):
        pl.semaphore_signal(semaphore, inc=1, device_id=to, device_id_type=mesh)

    def each(count, act):
        def step(d, carry):
            act(d)
            return carry

        lax.fori_loop(1, count, step, 0)

    far = sorted(range(1, nz), key=lambda d: -min(d, nz - d))

    turns_z = far + [0]
    turns = sorted(range(1, ny), key=lambda d: -min(d, ny - d)) + [0]
    fore = side // 2

    fetch = [
        pltpu.make_async_copy(src, dst, local_s.at[k])
        for k, (src, dst) in enumerate(
            (
                (members_hbm, members),
                (points_hbm.at[:, pl.ds(pl.multiple_of(y * 2 * TILE, 2 * TILE), 2 * TILE)], points),
                (labels_hbm, labels),
                (noise_hbm, noise),
                (observed_hbm, observed),
                (perturb_hbm, perts.at[z]),
                (alphas_hbm, alphas),
            )
        )
    ]
    for f in fetch:
        f.start()

    barrier = pltpu.get_barrier_semaphore()
    reach = range(1, nz // 4 + 1)
    near = [in_z(z_at(s * k % nz)) for k in reach for s in (1, -1)]
    each(no, lambda d: tell(barrier, (g, obs_at(d))))
    each(NX, lambda d: tell(barrier, in_x(x_at(d))))
    for to in near:
        tell(barrier, to)

    fetch[0].wait()
    own = members[...].astype(F32)
    for h in range(2):
        part = own[:, h * half : (h + 1) * half]
        rows_out[h] = jnp.concatenate([part[:, :quarter], part[:, quarter:]], axis=0).astype(BF16)
    rows_in[o] = rows_out[c]
    for k in range(nz):
        part = own[:, k * width : (k + 1) * width]
        blocks_out[k] = jnp.concatenate([part[:, : width // 2], part[:, width // 2 :]], axis=0).astype(BF16)
    blocks_in[z] = blocks_out[z]

    pl.semaphore_wait(barrier, no - 1 + NX - 1 + len(near))

    def rows_to(d):
        to = obs_at(d)
        return copy(rows_out.at[lax.rem(to, 2)], rows_in.at[o], rows_s.at[d], rows_r.at[o], (g, to))

    def rows_from(d):
        at = obs_at(d)
        return copy(rows_out.at[c], rows_in.at[at], rows_s.at[d], rows_r.at[at], (g, at))

    for d in sorted(range(1, no), key=lambda d: -min(d, no - d)):
        rows_to(d).start()
    for to in near[-2:]:
        tell(ready, to)

    fetch[1].wait()

    def tabulate(t):
        at = points[:, t * TILE : (t + 1) * TILE]
        turned = jnp.concatenate([at, jnp.zeros((TILE - at.shape[0], TILE), F32)], axis=0).T
        for d in range(at.shape[0]):
            value = jnp.broadcast_to(turned[:, d : d + 1], (TILE, TILE))
            second = value * value - 1.0
            third = value * second - 2.0 * value
            table[t, d, 0] = value
            table[t, d, 1] = second * (1.0 / math.sqrt(2.0))
            table[t, d, 2] = third * (1.0 / math.sqrt(6.0))

    tabulate(0)
    tabulate(1)

    for f in fetch[2:]:
        f.wait()
    label = jnp.broadcast_to(labels[...].astype(F32), (TILE, TILE))
    diagonal = lax.broadcasted_iota(jnp.int32, (TILE, TILE), 0) == lax.broadcasted_iota(jnp.int32, (TILE, TILE), 1)
    coupled[...] = jnp.where(label == label.T, 1.0 / (ensemble - 1), 0.0).astype(F32)
    spread[...] = jnp.where(diagonal, jnp.broadcast_to(noise[...], (TILE, TILE)), 0.0)

    def basis_part(first_step, last_step):
        def step(n, carry):
            per = quarter // chunk
            q, t, k = lax.div(n, 2 * per), lax.rem(lax.div(n, per), 2), lax.rem(n, per)
            first = pl.multiple_of(k * chunk, chunk)
            degree = alphas[:, pl.ds(pl.multiple_of(c * half + q * quarter + first, chunk), chunk)]
            product = None
            for d in range(degree.shape[0]):
                odd = (degree[d : d + 1] & 1) == 1
                high = degree[d : d + 1] >= 2
                one, two, three = (jnp.concatenate([table[t, d, p]] * (chunk // TILE), axis=1) for p in range(3))
                value = jnp.where(high, jnp.where(odd, three, two), jnp.where(odd, one, 1.0))
                product = value if product is None else product * value
            place = pl.multiple_of((q * 2 + t) * TILE, TILE)
            basis[pl.ds(place, TILE), pl.ds(first, chunk)] = product.astype(BF16)
            return carry

        lax.fori_loop(first_step, last_step, step, 0)

    steps = 4 * (quarter // chunk)
    basis_part(0, steps // 8)
    pl.semaphore_wait(ready, 2)

    def block_to(d):
        return copy(blocks_out.at[z_at(d)], blocks_in.at[z], blocks_s.at[d], blocks_r.at[z], in_z(z_at(d)))

    def block_from(d):
        at = z_at(d)
        return copy(blocks_out.at[at], blocks_in.at[at], blocks_s.at[d], blocks_r.at[at], in_z(at))

    def pert_to(d):
        return copy(perts.at[z], perts.at[z], perts_s.at[d], perts_r.at[z], in_z(z_at(d)))

    def pert_from(d):
        at = z_at(d)
        return copy(perts.at[at], perts.at[at], perts_s.at[d], perts_r.at[at], in_z(at))

    for d in far:
        block_to(d).start()
    basis_part(steps // 8, steps)

    each(no, lambda d: rows_from(d).wait_recv())
    both = dot(rows_in[...].reshape(no * 2 * ROWS, quarter), basis[...], LAST)
    both = both.reshape(no, 2, ROWS, 4 * TILE)
    part = (both[:, 0, :, : 2 * TILE] + both[:, 1, :, 2 * TILE :]).reshape(no * ROWS, 2 * TILE)
    for t in range(2):
        halves[t] = part[:, t * TILE : (t + 1) * TILE]
    half_copy = copy(halves.at[1 - c], half_in, half_s, half_r, (g, sibling))
    half_copy.start()
    half_copy.wait_recv()
    preds[z] = (halves[c] + half_in[...]).astype(BF16)

    def pred_to(d):
        return copy(preds.at[z], preds.at[z], preds_s.at[d], preds_r.at[z], in_z(z_at(d)))

    def pred_from(d):
        at = z_at(d)
        return copy(preds.at[at], preds.at[at], preds_s.at[d], preds_r.at[at], in_z(at))

    for d in far:
        pred_to(d).start()

    each(nz, lambda d: block_from(d).wait_recv())
    block = blocks_in[...].astype(F32)
    block = jnp.concatenate([block[:, :ROWS], block[:, ROWS:]], axis=2)
    slabs[o] = block.reshape(side, width).astype(BF16)

    def slab_to(d):
        return copy(slabs.at[o], slabs.at[o], slabs_s.at[d], slabs_r.at[o], (g, y_at(d) * 2 + c))

    def slab_from(at, to):
        return copy(slabs.at[at], slabs.at[at], slabs_s.at[0], slabs_r.at[at], (g, to))

    def slab_pass(d):
        at = y_at(d) * 2 + c
        return copy(slabs.at[at], slabs.at[at], slabs_s.at[ny + d], slabs_r.at[at], (g, sibling))

    slab_own = copy(slabs.at[o], slabs.at[o], slabs_s.at[0], slabs_r.at[o], (g, sibling))
    slab_own.start()
    for d in turns[:-1]:
        slab_to(d).start()

    def pass_on(d):
        at = y_at(d) * 2 + c
        slab_from(at, at).wait_recv()
        slab_pass(d).start()

    for d in reversed(turns[:-1]):
        pass_on(d)

    each(nz, lambda d: pred_from(d).wait_recv())
    flat = preds[...].reshape(line, TILE)
    ones = jnp.ones((2 * ROWS, line), BF16)
    gram = dot(flat, flat, FIRST)
    grams[x] = jnp.concatenate([folded(gram), dot(ones, flat, PLAIN)[:ROWS], diagonal_row(gram)], axis=0)

    def gram_to(d):
        return copy(grams.at[x], grams.at[x], grams_s.at[d], grams_r.at[x], in_x(x_at(d)))

    def gram_from(d):
        at = x_at(d)
        return copy(grams.at[at], grams.at[at], grams_s.at[d], grams_r.at[at], in_x(at))

    for d in sorted(range(1, NX), key=lambda d: -min(d, NX - d)):
        gram_to(d).start()
    for d in far:
        pert_to(d).start()

    for t in range(nz):
        value = preds[t].astype(F32)
        for k in range(no):
            prior[k, t * ROWS : (t + 1) * ROWS, :] = value[k * ROWS : (k + 1) * ROWS]
    ordered = prior[...].reshape(line, TILE).astype(BF16)

    slab_from(sibling, sibling).wait_recv()
    each(ny, lambda d: slab_from(y_at(d) * 2 + 1 - c, sibling).wait_recv())
    slab = slabs[...].reshape(line, width)
    raw = dot(ordered, slab, FIRST)
    total = dot(ones, slab, PLAIN)[:ROWS]
    for k in range(NX):
        cross_out[k, :ROWS] = total[:, k * SLAB : (k + 1) * SLAB]
        cross_out[k, ROWS:] = raw[:, k * SLAB : (k + 1) * SLAB]
    cross_in[x] = cross_out[x]

    def piece(h):
        return pl.ds(h * (TILE // 2 + ROWS), TILE // 2 + ROWS * (1 - h))

    def cross_to(d, h):
        at = x_at(d)
        return copy(cross_out.at[at, piece(h)], cross_in.at[x, piece(h)], cross_s.at[d, h], cross_r.at[x, h], in_x(at))

    def cross_from(d, h):
        at = x_at(d)
        return copy(cross_out.at[at, piece(h)], cross_in.at[at, piece(h)], cross_s.at[d, h], cross_r.at[at, h], in_x(at))

    for h in range(2):
        for d in sorted(range(1, NX), key=lambda d: -min(d, NX - d)):
            cross_to(d, h).start()

    each(NX, lambda d: gram_from(d).wait_recv())
    gram = grams[0]
    for k in range(1, NX):
        gram = gram + grams[k]
    mean_pred = jnp.broadcast_to(gram[TILE // 2 : TILE // 2 + 1] / ensemble, (TILE, TILE))
    mean_turned = mean_pred.T
    gram = unfolded(gram[: TILE // 2], gram[TILE // 2 + ROWS :])
    system = (gram - ensemble * mean_turned * mean_pred) * coupled[...] + spread[...]

    inverted = inverse_blocks(system, 0, TILE // PANEL // 4)

    def crosses_to(d, h):
        span = crosses.at[x, pl.ds(h * TILE // 2, TILE // 2)]
        return copy(span, span, crosses_s.at[d, h], crosses_r.at[x, h], in_x(x_at(d)))

    def crosses_from(d, h):
        at = x_at(d)
        span = crosses.at[at, pl.ds(h * TILE // 2, TILE // 2)]
        return copy(span, span, crosses_s.at[d, h], crosses_r.at[at, h], in_x(at))

    mean_param = None
    for h in range(2):
        for d in range(1, NX):
            cross_from(d, h).wait_recv()
        cross = cross_in[0, piece(h)]
        for k in range(1, NX):
            cross = cross + cross_in[k, piece(h)]
        if h == 0:
            mean_param = cross[:1] / ensemble
            cross = cross[ROWS:]
        part = slice(h * TILE // 2, (h + 1) * TILE // 2)
        crosses[x, part] = cross - ensemble * mean_turned[part] * mean_param
        for d in sorted(range(1, NX), key=lambda d: -min(d, NX - d)):
            crosses_to(d, h).start()
        if h == 0:
            inverted = inverse_blocks(inverted, TILE // PANEL // 4, TILE // PANEL // 2)

    each(nz, lambda d: pert_from(d).wait_recv())
    noise_root = jnp.sqrt(noise[...])
    for t, d in enumerate(turns_z):
        at = z_at(d)
        left = observed[...] + noise_root * perts[at].astype(F32) - preds[at].astype(F32)
        for k in range(no):
            innov[k % 2, k // 2, t * ROWS : (t + 1) * ROWS, :] = left[k * ROWS : (k + 1) * ROWS]

    inverted = inverse_blocks(inverted, TILE // PANEL // 2, TILE // PANEL)

    for h in range(2):
        for d in range(1, NX):
            crosses_from(d, h).wait_recv()
    cross = jnp.concatenate([crosses[k] for k in range(NX)], axis=1)
    gain = dot(inverted, cross, PLAIN, lax.Precision.HIGHEST) / (ensemble - 1)
    high = gain.astype(BF16)
    low = (gain - high.astype(F32)).astype(BF16)
    weights = jnp.concatenate([high, low], axis=1)
    weights = jnp.concatenate([weights, weights], axis=0)

    def share(core, d):
        left = innov[core, y_at(d)]
        big = left.astype(BF16)
        small = (left - big.astype(F32)).astype(BF16)
        parts = dot(jnp.concatenate([big, small], axis=1), weights, PLAIN)
        return parts[:, :width] + parts[:, width:]

    def pair_copy(d):
        return copy(pair_out.at[d], pair_in.at[d], pair_s.at[d], pair_r.at[d], (g, sibling))

    def share_to(d, h):
        span = pl.ds(h * fore, fore)
        to = (g, y_at(d) * 2 + c)
        return copy(share_out.at[d, span], share_in.at[y, span], share_s.at[d, h], share_r.at[y, h], to)

    def share_from(d, h):
        at = y_at(d)
        span = pl.ds(h * fore, fore)
        return copy(share_out.at[d, span], share_in.at[at, span], share_s.at[d, h], share_r.at[at, h], (g, at * 2 + c))

    def incr_to(t):
        at = z_at(turns_z[t])
        return copy(incr_out.at[t], final.at[z], incr_s.at[t], incr_r.at[z], in_z(at))

    def incr_from(d):
        at = z_at(d)
        return copy(incr_out.at[0], final.at[at], incr_s.at[0], incr_r.at[at], in_z(at))

    for d in turns:
        pair_out[d] = share(1 - c, d).astype(BF16)
        pair_copy(d).start()
    mine = {d: share(c, d) for d in turns}
    for d in turns:
        pair_copy(d).wait_recv()
        total = mine[d] + pair_in[d].astype(F32)
        if d:
            share_out[d] = total.astype(BF16)
            share_to(d, 0).start()
    for d in turns[:-1]:
        share_to(d, 1).start()
    for h in range(2):
        part = total[h * fore : (h + 1) * fore]
        for d in turns[:-1]:
            share_from(d, h).wait_recv()
            part = part + share_in[y_at(d), h * fore : (h + 1) * fore].astype(F32)
        for t in range(h * nz // 2, (h + 1) * nz // 2):
            first = t * ROWS - h * fore
            incr_out[t] = part[first : first + ROWS]
            if t < nz - 1:
                incr_to(t).start()
    final[z] = incr_out[nz - 1]
    def y_sent(d):
        slab_to(d).wait_send()
        slab_pass(d).wait_send()
        share_to(d, 0).wait_send()
        share_to(d, 1).wait_send()
        pair_copy(d).wait_send()

    def z_sent(d):
        block_to(d).wait_send()
        pert_to(d).wait_send()
        pred_to(d).wait_send()

    def x_sent(d):
        gram_to(d).wait_send()
        for h in range(2):
            cross_to(d, h).wait_send()
            crosses_to(d, h).wait_send()

    each(no, lambda d: rows_to(d).wait_send())
    half_copy.wait_send()
    slab_own.wait_send()
    pair_copy(0).wait_send()
    each(ny, y_sent)
    each(nz, z_sent)
    for d in reversed(turns_z):
        at = z_at(d)
        if d:
            incr_from(d).wait_recv()
        place = pl.ds(pl.multiple_of(at * width, width), width)
        out[:, place] = members[:, place].astype(F32) + final[at]

    for t in range(nz - 1):
        incr_to(t).wait_send()
    each(NX, x_sent)


def shards(members, alphas, points, labels, noise, observed, perturb):
    nm, no = lax.axis_size("mem"), lax.axis_size("obs")
    nz, ny = nm // NX, no // 2
    coeffs = members.shape[1]
    dims = alphas.shape[0]
    side, width = nz * ROWS, coeffs // nz
    vmem, many = pltpu.VMEM, pltpu.SemaphoreType.DMA
    signal = pltpu.SemaphoreType.REGULAR
    return pl.pallas_call(
        lambda *refs: kernel(nm, no, *refs),
        out_shape=jax.ShapeDtypeStruct((ROWS, coeffs), F32),
        in_specs=[pl.BlockSpec(memory_space=pl.ANY)] * 7,
        out_specs=pl.BlockSpec(memory_space=vmem),
        scratch_shapes=[
            vmem((ROWS, coeffs), BF16),
            vmem((dims, coeffs), jnp.int32),
            vmem((dims, 2 * TILE), F32),
            vmem((1, TILE), jnp.int32),
            vmem((1, TILE), F32),
            vmem((1, TILE), F32),
            vmem((2, 2 * ROWS, coeffs // 4), BF16),
            vmem((no, 2 * ROWS, coeffs // 4), BF16),
            vmem((2, no * ROWS, TILE), F32),
            vmem((no * ROWS, TILE), F32),
            vmem((nz, 2 * ROWS, width // 2), BF16),
            vmem((nz, 2 * ROWS, width // 2), BF16),
            vmem((no, side, width), BF16),
            vmem((nz, no * ROWS, TILE), BF16),
            vmem((nz, no * ROWS, TILE), BF16),
            vmem((NX, TILE // 2 + 2 * ROWS, TILE), F32),
            vmem((2, dims, 3, TILE, TILE), F32),
            vmem((4 * TILE, coeffs // 4), BF16),
            vmem((2, ny, side, TILE), F32),
            vmem((no, side, TILE), F32),
            vmem((NX, TILE + ROWS, SLAB), F32),
            vmem((NX, TILE + ROWS, SLAB), F32),
            vmem((NX, TILE, SLAB), F32),
            vmem((ny, side, width), BF16),
            vmem((ny, side, width), BF16),
            vmem((ny, side, width), BF16),
            vmem((ny, side, width), BF16),
            vmem((nz, ROWS, width), F32),
            vmem((nz, ROWS, width), F32),
            vmem((TILE, TILE), F32),
            vmem((TILE, TILE), F32),
            signal,
            many((7,)),
            many((no,)),
            many((no,)),
            many,
            many,
            many((nz,)),
            many((nz,)),
            many((no,)),
            many((no,)),
            many((nz,)),
            many((nz,)),
            many((nz,)),
            many((nz,)),
            many((NX,)),
            many((NX,)),
            many((NX, 2)),
            many((NX, 2)),
            many((NX, 2)),
            many((NX, 2)),
            many((ny,)),
            many((ny,)),
            many((ny, 2)),
            many((ny, 2)),
            many((nz,)),
            many((nz,)),
        ],
        compiler_params=pltpu.CompilerParams(
            collective_id=0, has_side_effects=True, vmem_limit_bytes=60 * 1024 * 1024
        ),
    )(members, alphas, points, labels.reshape(1, TILE), noise.reshape(1, TILE), observed.reshape(1, TILE), perturb)


def solution(mesh):
    in_specs = (P(("mem", "obs"), None), P(), P(), P("obs"), P("obs"), P("obs"), P("mem", "obs"))
    out_specs = P(("mem", "obs"), None)
    return jax.shard_map(shards, mesh=mesh, in_specs=in_specs, out_specs=out_specs, check_vma=False)
```
